32 devices in a mesh: grp: 2 (over x), pts: 8 (over z, y), maps: 2 (over core).
Axes of the slice: x: 2, y: 2, z: 4, core: 2. Of those that a mesh axis runs over, the one named last changes fastest.
Arguments:
- features: bfloat16 [32768, 128], P(('grp', 'pts', 'maps')), parts along dimension 0, may hold values from -6 to 6
- target: bfloat16 [128, 32768], P('maps', ('grp', 'pts')), parts along dimension 1, may hold values from -6 to 6
- branch: bfloat16 [256, 1024], P(('grp', 'maps'), 'pts'), parts along dimension 0, may hold values from -6 to 6
- w_in: bfloat16 [1024, 128], P(('pts', 'maps')), may hold values from -0.5 to 0.5
- w_mid: bfloat16 [1024, 1024], P(('pts', 'maps')), may hold values from -0.1875 to 0.1875
- w_out: bfloat16 [1024, 1024], P(('pts', 'maps')), may hold values from -0.1875 to 0.1875
Outputs:
- grad_branch: float32 [1024, 256], P('pts', ('grp', 'maps')), parts along dimension 1
- grad_in: float32 [2048, 128], P(('grp', 'pts', 'maps')), parts along dimension 0
- grad_mid: float32 [2048, 1024], P(('grp', 'pts', 'maps')), parts along dimension 0
- grad_out: float32 [2048, 1024], P(('grp', 'pts', 'maps')), parts along dimension 0
The draws below stay inside these ranges and needn't reach their ends.
There are 2 independent parts, one for each index of `grp`. The reference program is written for one: setup_inputs(seed, part) draws one part's arguments, and reference() takes and returns one part's arrays. A program takes and returns all parts, laid end to end along the dimension named above; an argument that names none is the same for every part. Nothing has to cross between parts.
All inputs are finite; a program needn't handle non-finite values.
Results may differ from the reference program's by a relative error of at most 0.0016.
Values may be sent and summed in bfloat16 or wider, within the bound.
No kernel may reach another device: no remote copies, remote signals or barrier semaphores. Data moves between devices by JAX's collectives and lax.ppermute only.
A program may use at most 64 MiB of HBM per device.

```python
import math
import jax
import jax.numpy as jnp
from jax import lax

P_SIZE = 1024
H = 1024
E = 128
MAPS = 128
POINTS = 16384


def levels(rng, extent, cuts, smallest, largest):
    factor_of, own = 1.0, jax.random.fold_in(rng, 6)
    for axis_at, shards_of in cuts:
        draws = jnp.exp(jax.random.uniform(jax.random.fold_in(own, axis_at), (shards_of,), jnp.float32, smallest / len(cuts), largest / len(cuts)))
        factor_of = factor_of * jnp.repeat(draws, extent[axis_at] // shards_of).reshape([-1 if axis == axis_at else 1 for axis in range(len(extent))])
    return factor_of


def normal_values(stream_key, dims, deviation, reach, shards=(), dtype=jnp.bfloat16):
    loudness = levels(stream_key, dims, shards, -0.22, 0.18) if shards else 1.0
    result = jax.random.normal(stream_key, dims, jnp.float32) * deviation * loudness
    return jnp.minimum(jnp.maximum(result, -reach), reach).astype(dtype)


def setup_inputs(seed: int = 0, part: int = 0) -> dict:
    keys = jax.random.split(jax.random.key(seed), 7)
    part_keys = jax.random.split(jax.random.fold_in(keys[6], part), 7)
    features = normal_values(part_keys[0], (POINTS, E), 1.0, 6.0, ((0, 16),))
    target = normal_values(part_keys[1], (MAPS, POINTS), 1.0, 6.0, ((0, 2), (1, 8)))
    branch = normal_values(part_keys[2], (MAPS, P_SIZE), 1.0, 6.0, ((0, 2), (1, 8)))
    w_in = normal_values(keys[3], (H, E), E ** -0.5, 0.5, ((0, 16),))
    w_mid = normal_values(keys[4], (H, H), H ** -0.5, 0.1875, ((0, 16),))
    w_out = normal_values(keys[5], (H, P_SIZE), H ** -0.5, 0.1875, ((0, 16),))
    return dict(features=features, target=target, branch=branch, w_in=w_in, w_mid=w_mid, w_out=w_out)


def contract(left, right, left_dim, right_dim):
    return lax.dot_general(left, right, (((left_dim,), (right_dim,)), ((), ())), preferred_element_type=jnp.float32)

def contract_exact(left, right, left_dim, right_dim):
    return lax.dot_general(left.astype(jnp.float32), right.astype(jnp.float32), (((left_dim,), (right_dim,)), ((), ())), precision=lax.Precision.HIGHEST, preferred_element_type=jnp.float32)

def reference(features, target, branch, w_in, w_mid, w_out):
    scale_b = 1.0 / math.sqrt(branch.shape[1])
    scale_p = 1.0 / math.sqrt(target.shape[1])
    first = jnp.tanh(contract(features, w_in, 1, 1)).astype(jnp.bfloat16)
    second = jnp.tanh(jnp.dot(first, w_mid, preferred_element_type=jnp.float32)).astype(jnp.bfloat16)
    trunk = jnp.dot(second, w_out, preferred_element_type=jnp.float32).astype(jnp.bfloat16)
    field = contract(branch, trunk, 1, 1) * scale_b
    resid = (field - target.astype(jnp.float32)) * scale_p
    grad_branch = contract_exact(trunk, resid, 0, 1) * scale_b
    d_trunk = (contract_exact(resid, branch, 0, 0) * scale_b).astype(jnp.bfloat16)
    grad_out = contract(second, d_trunk, 0, 0)
    second_f = second.astype(jnp.float32)
    dz_second = (contract(d_trunk, w_out, 1, 1) * (1.0 - second_f * second_f)).astype(jnp.bfloat16)
    grad_mid = contract(first, dz_second, 0, 0)
    first_f = first.astype(jnp.float32)
    dz_first = (contract(dz_second, w_mid, 1, 1) * (1.0 - first_f * first_f)).astype(jnp.bfloat16)
    grad_in = contract(dz_first, features, 0, 0)
    return (grad_branch, grad_in, grad_mid, grad_out)
```

```python
import functools
import math

import jax
import jax.numpy as jnp
from jax import lax
from jax.experimental import pallas as pl
from jax.experimental.pallas import tpu as pltpu
from jax.sharding import PartitionSpec as P

BF = jnp.bfloat16
F32 = jnp.float32
VMEM_BYTES = 56 * 1024 * 1024


def dot(left, right, left_dim, right_dim):
    return lax.dot_general(
        left, right, (((left_dim,), (right_dim,)), ((), ())), preferred_element_type=F32
    )


def dot_exact(left, right, left_dim, right_dim):
    return lax.dot_general(
        left.astype(F32),
        right.astype(F32),
        (((left_dim,), (right_dim,)), ((), ())),
        precision=lax.Precision.HIGHEST,
        preferred_element_type=F32,
    )


def split(value):
    high = lax.reduce_precision(value, 8, 7)
    return high.astype(BF), (value - high).astype(BF)


def encode(value):
    return (value * value * value).astype(BF)


def decode(code):
    cube = code.astype(F32)
    size = jnp.abs(cube)
    root = jnp.exp2(jnp.log2(jnp.maximum(size, 1e-37)) * (1.0 / 3.0))
    return jnp.where(size < 1e-37, 0.0, jnp.where(cube < 0.0, -root, root))


def forward_kernel(features, near, far, first, second):
    half, width = near.shape[0], second.shape[1]
    x = features[...]
    f_near = jnp.tanh(dot(x, near[:, width:], 1, 1)).astype(BF)
    f_far = jnp.tanh(dot(x, far[:, width:], 1, 1)).astype(BF)
    first[:, :half] = f_near
    first[:, half:] = f_far
    z = dot(f_near, near[:, :width], 1, 0) + dot(f_far, far[:, :width], 1, 0)
    second[...] = jnp.tanh(z).astype(BF)


def middle_kernel(
    scale_p, features, first, second, near, far, target, b_high, b_low, total, dz, g_in
):
    half, width = near.shape[0], second.shape[1]

    @pl.when(pl.program_id(0) == 0)
    def _():
        total[...] = jnp.zeros_like(total)
        g_in[...] = jnp.zeros_like(g_in)

    maps = target.shape[1]
    s = second[...]
    bh, bl = b_high[...], b_low[...]
    field = dot(s, bh, 1, 0) + dot(s, bl, 1, 0)
    resid = (field - target[...].astype(F32)) * scale_p
    rh = resid.astype(BF)
    rl = (resid - rh.astype(F32)).astype(BF)
    both = dot(s, jnp.concatenate([rh, rl], axis=1), 0, 0)
    total[...] += both[:, :maps] + both[:, maps:]
    s32 = s.astype(F32)
    back = dot(rh, bh, 1, 1) + dot(rl, bh, 1, 1) + dot(rh, bl, 1, 1)
    d = (back * (1.0 - s32 * s32)).astype(BF)
    dz[...] = d
    f = first[...].astype(F32)
    slope = 1.0 - f * f
    x = features[...]
    d_near = (dot(d, near[:, :width], 1, 1) * slope[:, :half]).astype(BF)
    d_far = (dot(d, far[:, :width], 1, 1) * slope[:, half:]).astype(BF)
    g_in[:half, :] += dot(d_near, x, 0, 0)
    g_in[half:, :] += dot(d_far, x, 0, 0)


def grad_far_kernel(first, dz, g_in, out):
    width = dz.shape[1]
    g = dot(first[...], dz[...], 0, 0)
    out[:, :width] = encode(g)
    out[:, width:] = encode(g_in[...])


def grad_near_kernel(first, dz, g_in, out):
    width = dz.shape[1]
    out[:, :width] = dot(first[...], dz[...], 0, 0)
    out[:, width:] = g_in[...]


def cost(flops, moved):
    return pl.CostEstimate(flops=int(flops), bytes_accessed=int(moved), transcendentals=0)


def params():
    return pltpu.CompilerParams(vmem_limit_bytes=VMEM_BYTES)


def forward(features, near, far):
    points, enc = features.shape
    half, both = near.shape
    width = both - enc
    step = points // 4
    whole = pl.BlockSpec((half, both), lambda i: (0, 0))
    return pl.pallas_call(
        forward_kernel,
        grid=(points // step,),
        in_specs=[pl.BlockSpec((step, enc), lambda i: (i, 0)), whole, whole],
        out_specs=[
            pl.BlockSpec((step, 2 * half), lambda i: (i, 0)),
            pl.BlockSpec((step, width), lambda i: (i, 0)),
        ],
        out_shape=[
            jax.ShapeDtypeStruct((points, 2 * half), BF),
            jax.ShapeDtypeStruct((points, width), BF),
        ],
        compiler_params=params(),
        cost_estimate=cost(2 * points * 2 * half * both, 7e6),
    )(features, near, far)


def middle(scale_p, features, first, second, near, far, target, b_high, b_low):
    points, enc = features.shape
    half, both = near.shape
    width, maps = b_high.shape
    step = points // 4
    rows = lambda n: pl.BlockSpec((step, n), lambda i: (i, 0))
    whole = lambda a, b: pl.BlockSpec((a, b), lambda i: (0, 0))
    return pl.pallas_call(
        functools.partial(middle_kernel, scale_p),
        grid=(points // step,),
        in_specs=[
            rows(enc),
            rows(2 * half),
            rows(width),
            whole(half, both),
            whole(half, both),
            rows(maps),
            whole(width, maps),
            whole(width, maps),
        ],
        out_specs=[whole(width, maps), rows(width), whole(2 * half, enc)],
        out_shape=[
            jax.ShapeDtypeStruct((width, maps), F32),
            jax.ShapeDtypeStruct((points, width), BF),
            jax.ShapeDtypeStruct((2 * half, enc), F32),
        ],
        compiler_params=params(),
        cost_estimate=cost(2 * points * 2 * half * both * 1.8, 10e6),
    )(features, first, second, near, far, target, b_high, b_low)


def grad_half(first, dz, g_in, far):
    points, hidden = first.shape
    width, enc = dz.shape[1], g_in.shape[1]
    half = hidden // 2
    step = half // 2
    base = half // step if far else 0
    return pl.pallas_call(
        grad_far_kernel if far else grad_near_kernel,
        grid=(half // step,),
        in_specs=[
            pl.BlockSpec((points, step), lambda i: (0, i + base)),
            pl.BlockSpec((points, width), lambda i: (0, 0)),
            pl.BlockSpec((step, enc), lambda i: (i + base, 0)),
        ],
        out_specs=pl.BlockSpec((step, width + enc), lambda i: (i, 0)),
        out_shape=jax.ShapeDtypeStruct((half, width + enc), BF if far else F32),
        compiler_params=params(),
        cost_estimate=cost(2 * points * half * width, 6e6),
    )(first, dz, g_in)


def shift(n, mask):
    return [(i, i ^ mask) for i in range(n)]


def per_device(features, target, branch, w_in, w_mid, w_out):
    n_pts = lax.axis_size("pts")
    core = lax.axis_index("maps")
    rows, width = w_mid.shape
    hidden = rows * n_pts * 2
    maps = 2 * branch.shape[0]
    points, enc = features.shape
    scale_b = 1.0 / math.sqrt(width)
    scale_p = 1.0 / math.sqrt(target.shape[1] * n_pts)
    swap_core = lambda v: lax.ppermute(v, "maps", [(0, 1), (1, 0)])
    move = lambda v, mask: lax.ppermute(v, "pts", shift(n_pts, mask))

    pick = lambda flag, a, b: jnp.where(flag, a, b)
    first_core = core == 0

    own = jnp.concatenate([w_mid, w_in], axis=1)
    parts = [own] + [move(own, 2 * k) for k in range(1, n_pts // 2)]
    line = jnp.concatenate(parts, axis=0)
    near = jnp.concatenate([line, move(line, 1)], axis=0)
    far = swap_core(near)

    wide = lax.all_to_all(
        jnp.broadcast_to(branch[None], (n_pts, *branch.shape)), "pts", 0, 0, tiled=True
    )
    wide = wide.transpose(1, 0, 2).reshape(maps // 2, width)
    wide_other = swap_core(wide)
    branch_full = jnp.concatenate(
        [pick(first_core, wide, wide_other), pick(first_core, wide_other, wide)], axis=0
    )
    folded = dot(w_out, branch_full, 1, 1) * scale_b
    spread = lax.all_to_all(
        jnp.broadcast_to(folded[None], (n_pts, rows, maps)), "pts", 0, 0, tiled=True
    )
    other = swap_core(spread)
    b_t = jnp.stack(
        [pick(first_core, spread, other), pick(first_core, other, spread)], axis=1
    ).reshape(hidden, maps)
    b_high, b_low = split(b_t)

    t_own = lax.dynamic_slice_in_dim(target, core * points, points, 1)
    t_other = swap_core(lax.dynamic_slice_in_dim(target, (1 - core) * points, points, 1))
    t_full = jnp.concatenate(
        [pick(first_core, t_own, t_other), pick(first_core, t_other, t_own)], axis=0
    ).T

    first, second = forward(features, near, far)
    total, dz, g_in = middle(
        scale_p, features, first, second, near, far, t_full, b_high, b_low
    )
    send = grad_half(first, dz, g_in, True)
    keep = grad_half(first, dz, g_in, False)

    by_core = total.reshape(n_pts, 2, rows, maps)
    mine = lax.dynamic_index_in_dim(by_core, core, 1, keepdims=False)
    theirs = lax.dynamic_index_in_dim(by_core, 1 - core, 1, keepdims=False)
    mine = mine + swap_core(theirs)
    got = lax.all_to_all(encode(mine), "pts", 0, 0, tiled=True)
    sums = jnp.sum(decode(got), axis=0)
    grad_out = dot_exact(sums, branch_full, 1, 0) * scale_b
    part = dot_exact(sums, w_out, 0, 0) * scale_b
    part_mine = lax.dynamic_slice_in_dim(part, core * (maps // 2), maps // 2, 0)
    part_theirs = lax.dynamic_slice_in_dim(part, (1 - core) * (maps // 2), maps // 2, 0)
    part_mine = part_mine + swap_core(part_theirs)
    blocks = part_mine.reshape(maps // 2, n_pts, width // n_pts).transpose(1, 0, 2)
    got_b = lax.all_to_all(encode(blocks), "pts", 0, 0, tiled=True)
    grad_branch = jnp.sum(decode(got_b), axis=0).T

    both = keep + decode(swap_core(send))
    quarter = hidden // 4
    both = both[:quarter] + decode(move(encode(both[quarter:]), 1))
    chunk = lambda k: both[k * rows : (k + 1) * rows]
    grads = chunk(0)
    for k in range(1, n_pts // 2):
        grads = grads + decode(move(encode(chunk(k)), 2 * k))
    return (grad_branch, grads[:, width:], grads[:, :width], grad_out)


def solution(mesh):
    in_specs = (
        P(("grp", "pts", "maps"), None),
        P("maps", ("grp", "pts")),
        P(("grp", "maps"), "pts"),
        P(("pts", "maps"), None),
        P(("pts", "maps"), None),
        P(("pts", "maps"), None),
    )
    out_specs = (
        P("pts", ("grp", "maps")),
        P(("grp", "pts", "maps"), None),
        P(("grp", "pts", "maps"), None),
        P(("grp", "pts", "maps"), None),
    )
    return jax.shard_map(
        per_device, mesh=mesh, in_specs=in_specs, out_specs=out_specs, check_vma=False
    )
```

```python
import functools
import math

import jax
import jax.numpy as jnp
from jax import lax
from jax.experimental import pallas as pl
from jax.experimental.pallas import tpu as pltpu
from jax.sharding import PartitionSpec as P

BF = jnp.bfloat16
F32 = jnp.float32
MIB = 1024 * 1024
KERNEL_MIB = 44


def dot(left, right, left_dim, right_dim):
    return lax.dot_general(
        left, right, (((left_dim,), (right_dim,)), ((), ())), preferred_element_type=F32
    )


def split(value):
    high = value.astype(BF)
    return high, (value - high.astype(F32)).astype(BF)


def encode(value):
    return (value * value * value).astype(BF)


def decode(code):
    cube = code.astype(F32)
    size = jnp.abs(cube)
    root = jnp.exp2(jnp.log2(jnp.maximum(size, 1e-37)) * (1.0 / 3.0))
    return jnp.where(size < 1e-37, 0.0, jnp.where(cube < 0.0, -root, root))


def stack_kernel(*refs):
    *parts, out, small = refs
    rows, width = parts[0].shape[0], out.shape[1]
    for k, part in enumerate(parts):
        out[k * rows : (k + 1) * rows, :] = part[:, :width]
        small[k * rows : (k + 1) * rows, :] = part[:, width:]


def both_kernel(core_ref, own, other, after, out):
    rows = own.shape[0]
    zero = core_ref[0] == 0
    a, b = own[...], other[...]
    out[:rows] = jnp.where(zero, a, b)
    out[rows:] = jnp.where(zero, b, a)


def fold_branch_kernel(scale_b, place_ref, w_both, branch, out, wide):
    if branch.shape == wide.shape:
        wide[...] = branch[...]
    else:
        maps, n_pts = wide.shape[0], out.shape[0]
        each = branch.shape[1] // 2
        for j in range(n_pts):
            at = pl.multiple_of(place_ref[j] * each, each)
            wide[:, pl.ds(at, each)] = branch[j * maps : (j + 1) * maps, :each]
    code = encode(dot(wide[...], w_both[...], 1, 1) * scale_b)
    for p in range(out.shape[0]):
        out[p] = code


def main_kernel(
    scale_p, core_ref, features, small, small_other, near_a, near_b, far_a, far_b,
    b_own, b_other, target,
    far, near, s_mine, s_theirs, first_out, dz_out,
    first, second, dz, w_in, w_mid, pairs, b_all, branch, near_all, far_all, in_sem, out_sem,
):
    points, hidden = first.shape
    n_pts, rows, maps = s_mine.shape
    enc = features.shape[1]
    quarter, half, step = hidden // 4, hidden // 2, points // 4
    loads = [
        pltpu.make_async_copy(part, w_mid.at[pl.ds(j * quarter, quarter), :], in_sem.at[j])
        for j, part in enumerate((near_a, near_b, far_a, far_b))
    ]
    for load in loads:
        load.start()
    core = core_ref[0]
    w_in[:half, :] = small[:, enc:]
    w_in[half:, :] = small_other[:, enc:]
    for i in range(4):
        block = slice(i * step, (i + 1) * step)
        first[block, :] = jnp.tanh(dot(features[block, :], w_in[...], 1, 1)).astype(BF)
    save_first = pltpu.make_async_copy(first, first_out, out_sem.at[0])
    save_first.start()
    few = maps // 2
    for p in range(n_pts):
        cols = slice(2 * p * rows, 2 * (p + 1) * rows)
        branch[pl.ds(core * few, few), cols] = decode(b_own[p])
        branch[pl.ds((1 - core) * few, few), cols] = decode(b_other[p])
    bh, bl = split(branch[...])
    b_pair = jnp.concatenate([bh, bl], axis=0)
    b_three = jnp.concatenate([bh, bh, bl], axis=0)
    for load in loads:
        load.wait()
    for i in range(4):
        block = slice(i * step, (i + 1) * step)
        s = jnp.tanh(dot(first[block, :], w_mid[...], 1, 0)).astype(BF)
        second[block, :] = s
        pair = dot(s, b_pair, 1, 1)
        field = pair[:, :maps] + pair[:, maps:]
        resid = (field - target[block, :].astype(F32)) * scale_p
        rh, rl = split(resid)
        pairs[block, :] = jnp.concatenate([rh, rl], axis=1)
        s32 = s.astype(F32)
        back = dot(jnp.concatenate([rh, rl, rh], axis=1), b_three, 1, 0)
        dz[block, :] = (back * (1.0 - s32 * s32)).astype(BF)
    save_dz = pltpu.make_async_copy(dz, dz_out, out_sem.at[1])
    save_dz.start()
    both = dot(second[...], pairs[...], 0, 0)
    b_all[...] = both[:, :maps] + both[:, maps:]
    for p in range(n_pts):
        at = 2 * p * rows
        s_mine[p] = b_all[pl.ds(at + core * rows, rows), :]
        s_theirs[p] = encode(b_all[pl.ds(at + (1 - core) * rows, rows), :])
    saves = [save_first, save_dz]
    for i in range(4):
        block = slice(i * quarter, (i + 1) * quarter)
        g = dot(first[:, block], dz[...], 0, 0)
        if i < 2:
            source, target_ref, part = near_all, near, block
            near_all[part, :] = g
        else:
            source, target_ref, part = far_all, far, slice((i - 2) * quarter, (i - 1) * quarter)
            far_all[part, :] = encode(g)
        saves.append(
            pltpu.make_async_copy(source.at[part, :], target_ref.at[part, :], out_sem.at[2 + i])
        )
        saves[-1].start()
    for save in saves:
        save.wait()


def send_kernel(near, got, low):
    quarter = low.shape[0]
    low[...] = encode(near[quarter:] + decode(got[quarter:]))


def keep_kernel(near, got, after, own):
    quarter = own.shape[0]
    own[...] = near[:quarter] + decode(got[:quarter])


def pack_sums_kernel(mine, got, after, out):
    out[...] = encode(mine[...] + decode(got[...]))


def sums_kernel(scale_b, core_ref, got, own, other, w_out, after, grad_out, mine, theirs):
    total = decode(got[0])
    for p in range(1, got.shape[0]):
        total += decode(got[p])
    sh, sl = split(total)
    w = w_out[...]
    zero = core_ref[0] == 0
    top, bottom = jnp.where(zero, own[...], other[...]), jnp.where(zero, other[...], own[...])
    b = jnp.concatenate([top, bottom], axis=0)
    grad_out[...] = (dot(sh, b, 1, 0) + dot(sl, b, 1, 0)) * scale_b
    part = (dot(sh, w, 0, 0) + dot(sl, w, 0, 0)) * scale_b
    half = part.shape[0] // 2
    mine[...] = jnp.where(zero, part[:half], part[half:])
    theirs[...] = encode(jnp.where(zero, part[half:], part[:half]))


def input_kernel(
    place_ref, features_in, first_in, near_a, near_b, far_a, far_b, dz_in, after, mine, theirs,
    features, grads, first, w_mid, dz, sem,
):
    points, hidden = first.shape
    quarter, half, step = hidden // 4, hidden // 2, points // 4
    weights = [
        pltpu.make_async_copy(part, w_mid.at[pl.ds(j * quarter, quarter), :], sem.at[j])
        for j, part in enumerate((near_a, near_b, far_a, far_b))
    ]
    block = lambda i: slice(i * step, (i + 1) * step)
    values = [
        [
            pltpu.make_async_copy(source.at[block(i), :], to.at[block(i), :], sem.at[4 + 2 * i + k])
            for k, (source, to) in enumerate(((dz_in, dz), (first_in, first)))
        ]
        for i in range(4)
    ]
    load_features = pltpu.make_async_copy(features_in, features, sem.at[12])
    for load in (values[0][0], weights[0], values[0][1], *weights[1:]):
        load.start()
    for load in (*values[1], *values[2], *values[3], load_features):
        load.start()
    for i in range(4):
        values[i][0].wait()
        values[i][1].wait()
        d = dz[block(i), :]
        for j in range(4):
            if i == 0:
                weights[j].wait()
            cols = slice(j * quarter, (j + 1) * quarter)
            f = first[block(i), cols].astype(F32)
            back = dot(d, w_mid[cols, :], 1, 1)
            grads[block(i), cols] = (back * (1.0 - f * f)).astype(BF)
    load_features.wait()
    g = dot(features[...], grads[...], 0, 0).T
    n_pts, rows, _ = mine.shape
    for j in range(n_pts):
        p = place_ref[j]
        mine[p] = g[j * rows : (j + 1) * rows]
        theirs[p] = encode(g[half + j * rows : half + (j + 1) * rows])


def pack_last_kernel(part, mine, got, after, out):
    enc = part.shape[2]
    out[:, :, :enc] = encode(part[...])
    out[:, :, enc:] = encode(mine[...] + decode(got[...]))


def fold_kernel(own, got, keep, *codes):
    rows = keep.shape[0]
    keep[...] = own[:rows] + decode(got[:rows])
    for k, code in enumerate(codes):
        block = slice((k + 1) * rows, (k + 2) * rows)
        code[...] = encode(own[block] + decode(got[block]))


def hold_kernel(value, after, out):
    out[...] = value[...]


def last_kernel(keep, *refs):
    *codes, grad_mid = refs
    total = keep[...]
    for code in codes:
        total += decode(code[...])
    grad_mid[...] = total


def last_small_kernel(got, grad_branch, grad_in):
    total = decode(got[0])
    for p in range(1, got.shape[0]):
        total += decode(got[p])
    enc = grad_in.shape[1]
    part = total[:, :enc]
    grad_branch[...] = part.T if grad_branch.shape != part.shape else part
    grad_in[...] = total[:, enc:]


def cost(flops, moved):
    return pl.CostEstimate(flops=int(flops), bytes_accessed=int(moved), transcendentals=0)


def call(kernel, outs, scratch, estimate, spaces, *args, mib=KERNEL_MIB):
    kinds = {"s": pltpu.SMEM, "v": pltpu.VMEM, "h": pltpu.HBM, "a": pl.ANY}
    specs = [pl.BlockSpec(memory_space=kinds[c]) for c in spaces]
    return pl.pallas_call(
        kernel,
        in_specs=specs[: len(args)],
        out_specs=specs[len(args) :],
        out_shape=[jax.ShapeDtypeStruct(shape, dtype) for shape, dtype in outs],
        scratch_shapes=scratch,
        compiler_params=pltpu.CompilerParams(vmem_limit_bytes=mib * MIB),
        cost_estimate=estimate,
    )(*args)


def per_device(features, target, branch, w_in, w_mid, w_out):
    n_pts = lax.axis_size("pts")
    core = lax.axis_index("maps")
    point = lax.axis_index("pts")
    rows, width = w_mid.shape
    hidden = rows * n_pts * 2
    quarter, half = hidden // 4, hidden // 2
    n_hi = n_pts // 2
    maps = 2 * branch.shape[0]
    points, enc = features.shape
    scale_b = 1.0 / math.sqrt(width)
    scale_p = 1.0 / math.sqrt(target.shape[1] * n_pts)
    swap_core = lambda v: lax.ppermute(v, "maps", [(0, 1), (1, 0)])
    move = lambda v, mask: lax.ppermute(v, "pts", [(i, i ^ mask) for i in range(n_pts)])
    exchange = lambda v: lax.all_to_all(v, "pts", 0, 0, tiled=True)
    pick = lambda flag, a, b: jnp.where(flag, a, b)
    first_core = core == 0
    core_ref = core.reshape(1)
    masks = [2 * k + y for y in range(2) for k in range(n_hi)]
    place = point ^ jnp.array(masks, jnp.int32)

    own = jnp.concatenate([w_mid, branch.reshape(rows, enc), w_in], axis=1)
    parts = [own] + [move(own, 2 * k) for k in range(1, n_hi)]
    line, small = call(
        stack_kernel, [((quarter, width), BF), ((quarter, 2 * enc), BF)], [], cost(1, 1e6),
        "v" * n_hi + "vv", *parts,
    )
    small = jnp.concatenate([small, move(small, 1)], axis=0)
    small_other = swap_core(small)
    other = move(line, 1)
    mid = (line, other, swap_core(line), swap_core(other))
    square = width // n_pts == enc
    unmask = point ^ jnp.arange(n_pts, dtype=jnp.int32)
    unmask = (unmask % 2) * n_hi + unmask // 2
    wide = lambda v: (
        v[:, :enc].reshape(n_pts, *branch.shape)[unmask].transpose(1, 0, 2)
    ).reshape(maps // 2, width)
    wide_own = None if square else wide(small)

    (w_both,) = call(
        both_kernel, [((2 * rows, width), BF)], [], cost(5e10, 1), "svva" + "v",
        core_ref, w_out, swap_core(w_out), line,
    )
    folded, wide_own = call(
        functools.partial(fold_branch_kernel, scale_b),
        [((n_pts, maps // 2, 2 * rows), BF), ((maps // 2, width), BF)], [],
        cost(1, 1), "svv" + "vv", place, w_both, small if square else wide_own,
    )
    b_own = exchange(folded)
    b_other = swap_core(b_own)
    wide_other = swap_core(wide_own)

    t_own = lax.dynamic_slice_in_dim(target, core * points, points, 1)
    t_other = swap_core(lax.dynamic_slice_in_dim(target, (1 - core) * points, points, 1))
    t_full = jnp.concatenate(
        [pick(first_core, t_own, t_other), pick(first_core, t_other, t_own)], axis=0
    ).T

    dma = pltpu.SemaphoreType.DMA
    far, near, s_mine, s_theirs, first, dz = call(
        functools.partial(main_kernel, scale_p),
        [((half, width), BF), ((half, width), F32), ((n_pts, rows, maps), F32)]
        + [((n_pts, rows, maps), BF), ((points, hidden), BF), ((points, width), BF)],
        [
            pltpu.VMEM((points, hidden), BF), pltpu.VMEM((points, width), BF),
            pltpu.VMEM((points, width), BF), pltpu.VMEM((hidden, enc), BF),
            pltpu.VMEM((hidden, width), BF), pltpu.VMEM((points, 2 * maps), BF),
            pltpu.VMEM((width, maps), F32), pltpu.VMEM((maps, width), F32),
            pltpu.VMEM((half, width), F32), pltpu.VMEM((half, width), BF),
            dma((4,)), dma((6,)),
        ],
        cost(5e10, 8e6), "svvvhhhhvvv" + "hhvvhh",
        core_ref, features, small, small_other, *mid, b_own, b_other, t_full,
        mib=56,
    )

    far_got = swap_core(far)
    (low,) = call(
        send_kernel, [((quarter, width), BF)], [], cost(1, 1), "vv" + "v", near, far_got
    )
    (own,) = call(
        keep_kernel, [((quarter, width), F32)], [], cost(5e10, 1e6), "vva" + "v", near, far_got, low
    )

    (s_code,) = call(
        pack_sums_kernel, [((n_pts, rows, maps), BF)], [], cost(1, 1), "vva" + "v",
        s_mine, swap_core(s_theirs), own,
    )
    in_mine, in_theirs = call(
        input_kernel, [((n_pts, rows, enc), F32), ((n_pts, rows, enc), BF)],
        [
            pltpu.VMEM((points, enc), BF), pltpu.VMEM((points, hidden), BF),
            pltpu.VMEM((points, hidden), BF), pltpu.VMEM((hidden, width), BF),
            pltpu.VMEM((points, width), BF), dma((13,)),
        ],
        cost(5e10, 8e6), "shhhhhhha" + "vv", place, features, first, *mid, dz, own,
        mib=58,
    )
    strip = (maps // 2, width)
    grad_out, p_mine, p_theirs = call(
        functools.partial(sums_kernel, scale_b), [((rows, width), F32), (strip, F32), (strip, BF)],
        [], cost(1, 1), "svvvva" + "vvv",
        core_ref, exchange(s_code), wide_own, wide_other, w_out, in_mine,
    )
    part = p_mine + decode(swap_core(p_theirs))
    part = part.reshape(maps // 2, n_pts, width // n_pts).transpose(1, 0, 2)
    part = part.reshape(n_pts, rows, enc)

    wide_row = (rows, width)
    keep, *codes = call(
        fold_kernel, [(wide_row, F32)] + [(wide_row, BF)] * (n_hi - 1), [], cost(1, 1),
        "vv" + "v" * n_hi, own, move(low, 1),
    )
    (keep,) = call(hold_kernel, [(wide_row, F32)], [], cost(5e10, 1), "va" + "v", keep, codes[0])
    (last,) = call(
        pack_last_kernel, [((n_pts, rows, 2 * enc), BF)], [], cost(1, 1), "vvva" + "v",
        part, in_mine, swap_core(in_theirs), keep,
    )
    (keep,) = call(hold_kernel, [(wide_row, F32)], [], cost(5e10, 1), "va" + "v", keep, last)
    codes = [move(code, 2 * (k + 1)) for k, code in enumerate(codes)]
    (grad_mid,) = call(
        last_kernel, [(wide_row, F32)], [], cost(1, 1), "v" * n_hi + "v", keep, *codes
    )
    grad_branch, grad_in = call(
        last_small_kernel, [((enc, rows) if square else (rows, enc), F32), ((rows, enc), F32)],
        [], cost(1, 1), "v" + "vv", exchange(last),
    )
    if not square:
        grad_branch = grad_branch.reshape(maps // 2, width // n_pts).T
    return (grad_branch, grad_in, grad_mid, grad_out)


def solution(mesh):
    in_specs = (
        P(("grp", "pts", "maps"), None),
        P("maps", ("grp", "pts")),
        P(("grp", "maps"), "pts"),
        P(("pts", "maps"), None),
        P(("pts", "maps"), None),
        P(("pts", "maps"), None),
    )
    out_specs = (
        P("pts", ("grp", "maps")),
        P(("grp", "pts", "maps"), None),
        P(("grp", "pts", "maps"), None),
        P(("grp", "pts", "maps"), None),
    )
    return jax.shard_map(
        per_device, mesh=mesh, in_specs=in_specs, out_specs=out_specs, check_vma=False
    )
```

```python
import functools
import math

import jax
import jax.numpy as jnp
from jax import lax
from jax.experimental import pallas as pl
from jax.experimental.pallas import tpu as pltpu
from jax.sharding import PartitionSpec as P

BF = jnp.bfloat16
F32 = jnp.float32
MIB = 1024 * 1024
KERNEL_MIB = 12


def dot(left, right, left_dim, right_dim):
    return lax.dot_general(
        left, right, (((left_dim,), (right_dim,)), ((), ())), preferred_element_type=F32
    )


def split(value):
    high = value.astype(BF)
    return high, (value - high.astype(F32)).astype(BF)


def encode(value):
    return (value * value * value).astype(BF)


def decode(code):
    cube = code.astype(F32)
    size = jnp.abs(cube)
    root = jnp.exp2(jnp.log2(jnp.maximum(size, 1e-37)) * (1.0 / 3.0))
    return jnp.where(size < 1e-37, 0.0, jnp.where(cube < 0.0, -root, root))


def beside_kernel(w_mid, branch, w_in, out):
    width, enc = w_mid.shape[1], w_in.shape[1]
    out[:, :width] = w_mid[...]
    out[:, width : width + enc] = branch[...]
    out[:, width + enc :] = w_in[...]


def stack_kernel(*refs):
    *parts, out, small = refs
    rows, width = parts[0].shape[0], out.shape[1]
    for k, part in enumerate(parts):
        out[k * rows : (k + 1) * rows, :] = part[:, :width]
        small[k * rows : (k + 1) * rows, :] = part[:, width:]


def both_kernel(core_ref, own, other, after, out):
    rows = own.shape[0]
    zero = core_ref[0] == 0
    a, b = own[...], other[...]
    out[:rows] = jnp.where(zero, a, b)
    out[rows:] = jnp.where(zero, b, a)


def fold_branch_kernel(scale_b, place_ref, w_both, branch, out, wide):
    if branch.shape == wide.shape:
        wide[...] = branch[...]
    else:
        maps, n_pts = wide.shape[0], out.shape[0]
        each = branch.shape[1] // 2
        for j in range(n_pts):
            at = pl.multiple_of(place_ref[j] * each, each)
            wide[:, pl.ds(at, each)] = branch[j * maps : (j + 1) * maps, :each]
    code = encode(dot(wide[...], w_both[...], 1, 1) * scale_b)
    for p in range(out.shape[0]):
        out[p] = code


def main_kernel(
    scale_p, core_ref, features, small, small_other, near_a, near_b, far_a, far_b,
    b_own, b_other, target,
    far, near, s_mine, s_theirs, first_out, dz_out,
    first, second, dz, w_in, w_mid, pairs, b_all, branch, far_all, in_sem, out_sem,
):
    points, hidden = first.shape
    n_pts, rows, maps = s_mine.shape
    enc = features.shape[1]
    quarter, half, step = hidden // 4, hidden // 2, points // 4
    loads = [
        pltpu.make_async_copy(part, w_mid.at[pl.ds(j * quarter, quarter), :], in_sem.at[j])
        for j, part in enumerate((near_a, near_b, far_a, far_b))
    ]
    for load in loads:
        load.start()
    core = core_ref[0]
    w_in[:half, :] = small[:, enc:]
    w_in[half:, :] = small_other[:, enc:]
    for i in range(4):
        block = slice(i * step, (i + 1) * step)
        first[block, :] = jnp.tanh(dot(features[block, :], w_in[...], 1, 1)).astype(BF)
    save_first = pltpu.make_async_copy(first, first_out, out_sem.at[0])
    save_first.start()
    few = maps // 2
    for p in range(n_pts):
        cols = slice(2 * p * rows, 2 * (p + 1) * rows)
        branch[pl.ds(core * few, few), cols] = decode(b_own[p])
        branch[pl.ds((1 - core) * few, few), cols] = decode(b_other[p])
    bh, bl = split(branch[...])
    b_pair = jnp.concatenate([bh, bl], axis=0)
    b_three = jnp.concatenate([bh, bh, bl], axis=0)
    for load in loads:
        load.wait()
    for i in range(4):
        block = slice(i * step, (i + 1) * step)
        s = jnp.tanh(dot(first[block, :], w_mid[...], 1, 0)).astype(BF)
        second[block, :] = s
        pair = dot(s, b_pair, 1, 1)
        field = pair[:, :maps] + pair[:, maps:]
        resid = (field - target[block, :].astype(F32)) * scale_p
        rh, rl = split(resid)
        pairs[block, :] = jnp.concatenate([rh, rl], axis=1)
        s32 = s.astype(F32)
        back = dot(jnp.concatenate([rh, rl, rh], axis=1), b_three, 1, 0)
        dz[block, :] = (back * (1.0 - s32 * s32)).astype(BF)
    save_dz = pltpu.make_async_copy(dz, dz_out, out_sem.at[1])
    save_dz.start()
    both = dot(second[...], pairs[...], 0, 0)
    b_all[...] = both[:, :maps] + both[:, maps:]
    for p in range(n_pts):
        at = 2 * p * rows
        s_mine[p] = b_all[pl.ds(at + core * rows, rows), :]
        s_theirs[p] = encode(b_all[pl.ds(at + (1 - core) * rows, rows), :])
    saves = [save_first, save_dz]
    for i in range(4):
        block = slice(i * quarter, (i + 1) * quarter)
        g = dot(first[:, block], dz[...], 0, 0)
        if i < 2:
            near[block, :] = g
            continue
        part = slice((i - 2) * quarter, (i - 1) * quarter)
        far_all[part, :] = encode(g)
        saves.append(
            pltpu.make_async_copy(far_all.at[part, :], far.at[part, :], out_sem.at[i])
        )
        saves[-1].start()
    for save in saves:
        save.wait()


def send_kernel(near, got, low):
    quarter = low.shape[0]
    low[...] = encode(near[quarter:] + decode(got[quarter:]))


def keep_kernel(near, got, after, own):
    quarter = own.shape[0]
    own[...] = near[:quarter] + decode(got[:quarter])


def pack_sums_kernel(mine, got, after, out):
    out[...] = encode(mine[...] + decode(got[...]))


def sums_kernel(scale_b, core_ref, got, own, other, w_out, after, grad_out, mine, theirs):
    total = decode(got[0])
    for p in range(1, got.shape[0]):
        total += decode(got[p])
    sh, sl = split(total)
    w = w_out[...]
    zero = core_ref[0] == 0
    top, bottom = jnp.where(zero, own[...], other[...]), jnp.where(zero, other[...], own[...])
    b = jnp.concatenate([top, bottom], axis=0)
    grad_out[...] = (dot(sh, b, 1, 0) + dot(sl, b, 1, 0)) * scale_b
    part = (dot(sh, w, 0, 0) + dot(sl, w, 0, 0)) * scale_b
    half = part.shape[0] // 2
    mine[...] = jnp.where(zero, part[:half], part[half:])
    theirs[...] = encode(jnp.where(zero, part[half:], part[:half]))


def input_kernel(
    place_ref, features_in, first_in, near_a, near_b, far_a, far_b, dz_in, after, mine, theirs,
    features, grads, first, w_mid, dz, sem,
):
    points, hidden = first.shape
    quarter, half, step = hidden // 4, hidden // 2, points // 4
    weights = [
        pltpu.make_async_copy(part, w_mid.at[pl.ds(j * quarter, quarter), :], sem.at[j])
        for j, part in enumerate((near_a, near_b, far_a, far_b))
    ]
    block = lambda i: slice(i * step, (i + 1) * step)
    values = [
        [
            pltpu.make_async_copy(source.at[block(i), :], to.at[block(i), :], sem.at[4 + 2 * i + k])
            for k, (source, to) in enumerate(((dz_in, dz), (first_in, first)))
        ]
        for i in range(4)
    ]
    load_features = pltpu.make_async_copy(features_in, features, sem.at[12])
    for load in (values[0][0], weights[0], values[0][1], *weights[1:]):
        load.start()
    for load in (*values[1], *values[2], *values[3], load_features):
        load.start()
    for i in range(4):
        values[i][0].wait()
        values[i][1].wait()
        d = dz[block(i), :]
        for j in range(4):
            if i == 0:
                weights[j].wait()
            cols = slice(j * quarter, (j + 1) * quarter)
            f = first[block(i), cols].astype(F32)
            back = dot(d, w_mid[cols, :], 1, 1)
            grads[block(i), cols] = (back * (1.0 - f * f)).astype(BF)
    load_features.wait()
    g = dot(features[...], grads[...], 0, 0).T
    n_pts, rows, _ = mine.shape
    for j in range(n_pts):
        p = place_ref[j]
        mine[p] = g[j * rows : (j + 1) * rows]
        theirs[p] = encode(g[half + j * rows : half + (j + 1) * rows])


def pack_last_kernel(part, mine, got, after, out):
    enc = part.shape[2]
    out[:, :, :enc] = encode(part[...])
    out[:, :, enc:] = encode(mine[...] + decode(got[...]))


def fold_kernel(own, got, keep, *codes):
    rows = keep.shape[0]
    keep[...] = own[:rows] + decode(got[:rows])
    for k, code in enumerate(codes):
        block = slice((k + 1) * rows, (k + 2) * rows)
        code[...] = encode(own[block] + decode(got[block]))


def hold_kernel(value, after, out):
    out[...] = value[...]


def last_kernel(keep, *refs):
    *codes, grad_mid = refs
    total = keep[...]
    for code in codes:
        total += decode(code[...])
    grad_mid[...] = total


def last_small_kernel(got, grad_branch, grad_in):
    total = decode(got[0])
    for p in range(1, got.shape[0]):
        total += decode(got[p])
    enc = grad_in.shape[1]
    grad_branch[...] = total[:, :enc]
    grad_in[...] = total[:, enc:]


def cost(flops, moved):
    return pl.CostEstimate(flops=int(flops), bytes_accessed=int(moved), transcendentals=0)


def call(kernel, outs, scratch, estimate, spaces, *args, mib=KERNEL_MIB):
    kinds = {"s": pltpu.SMEM, "v": pltpu.VMEM, "h": pltpu.HBM, "a": pl.ANY}
    specs = [pl.BlockSpec(memory_space=kinds[c]) for c in spaces]
    return pl.pallas_call(
        kernel,
        in_specs=specs[: len(args)],
        out_specs=specs[len(args) :],
        out_shape=[jax.ShapeDtypeStruct(shape, dtype) for shape, dtype in outs],
        scratch_shapes=scratch,
        compiler_params=pltpu.CompilerParams(vmem_limit_bytes=mib * MIB),
        cost_estimate=estimate,
    )(*args)


def per_device(features, target, branch, w_in, w_mid, w_out):
    n_pts = lax.axis_size("pts")
    core = lax.axis_index("maps")
    point = lax.axis_index("pts")
    rows, width = w_mid.shape
    hidden = rows * n_pts * 2
    quarter, half = hidden // 4, hidden // 2
    n_hi = n_pts // 2
    maps = 2 * branch.shape[0]
    points, enc = features.shape
    scale_b = 1.0 / math.sqrt(width)
    scale_p = 1.0 / math.sqrt(target.shape[1] * n_pts)
    swap_core = lambda v: lax.ppermute(v, "maps", [(0, 1), (1, 0)])
    move = lambda v, mask: lax.ppermute(v, "pts", [(i, i ^ mask) for i in range(n_pts)])
    exchange = lambda v: lax.all_to_all(v, "pts", 0, 0, tiled=True)
    pick = lambda flag, a, b: jnp.where(flag, a, b)
    first_core = core == 0
    core_ref = core.reshape(1)
    masks = [2 * k + y for y in range(2) for k in range(n_hi)]
    place = point ^ jnp.array(masks, jnp.int32)

    (own,) = call(
        beside_kernel, [((rows, width + 2 * enc), BF)], [], cost(1, 1), "vvv" + "v",
        w_mid, branch.reshape(rows, enc), w_in,
    )
    parts = [own] + [move(own, 2 * k) for k in range(1, n_hi)]
    line, small = call(
        stack_kernel, [((quarter, width), BF), ((quarter, 2 * enc), BF)], [], cost(1, 1e6),
        "v" * n_hi + "vv", *parts,
    )
    small = jnp.concatenate([small, move(small, 1)], axis=0)
    small_other = swap_core(small)
    other = move(line, 1)
    mid = (line, other, swap_core(line), swap_core(other))
    square = width // n_pts == enc
    unmask = point ^ jnp.arange(n_pts, dtype=jnp.int32)
    unmask = (unmask % 2) * n_hi + unmask // 2
    wide = lambda v: (
        v[:, :enc].reshape(n_pts, *branch.shape)[unmask].transpose(1, 0, 2)
    ).reshape(maps // 2, width)
    wide_own = None if square else wide(small)

    (w_both,) = call(
        both_kernel, [((2 * rows, width), BF)], [], cost(5e10, 1), "svva" + "v",
        core_ref, w_out, swap_core(w_out), line,
    )
    folded, wide_own = call(
        functools.partial(fold_branch_kernel, scale_b),
        [((n_pts, maps // 2, 2 * rows), BF), ((maps // 2, width), BF)], [],
        cost(1, 1), "svv" + "vv", place, w_both, small if square else wide_own,
    )
    b_own = exchange(folded)
    b_other = swap_core(b_own)
    wide_other = swap_core(wide_own)

    t_own = lax.dynamic_slice_in_dim(target, core * points, points, 1)
    t_other = swap_core(lax.dynamic_slice_in_dim(target, (1 - core) * points, points, 1))
    t_full = jnp.concatenate(
        [pick(first_core, t_own, t_other), pick(first_core, t_other, t_own)], axis=0
    ).T

    dma = pltpu.SemaphoreType.DMA
    far, near, s_mine, s_theirs, first, dz = call(
        functools.partial(main_kernel, scale_p),
        [((half, width), BF), ((half, width), F32), ((n_pts, rows, maps), F32)]
        + [((n_pts, rows, maps), BF), ((points, hidden), BF), ((points, width), BF)],
        [
            pltpu.VMEM((points, hidden), BF), pltpu.VMEM((points, width), BF),
            pltpu.VMEM((points, width), BF), pltpu.VMEM((hidden, enc), BF),
            pltpu.VMEM((hidden, width), BF), pltpu.VMEM((points, 2 * maps), BF),
            pltpu.VMEM((width, maps), F32), pltpu.VMEM((maps, width), F32),
            pltpu.VMEM((half, width), BF), dma((4,)), dma((4,)),
        ],
        cost(5e10, 8e6), "svvvhhhhvvv" + "hvvvhh",
        core_ref, features, small, small_other, *mid, b_own, b_other, t_full,
        mib=44,
    )

    far_got = swap_core(far)
    (low,) = call(
        send_kernel, [((quarter, width), BF)], [], cost(1, 1), "vv" + "v", near, far_got
    )
    (own,) = call(
        keep_kernel, [((quarter, width), F32)], [], cost(5e10, 1e6), "vva" + "v", near, far_got, low
    )

    (s_code,) = call(
        pack_sums_kernel, [((n_pts, rows, maps), BF)], [], cost(1, 1), "vva" + "v",
        s_mine, swap_core(s_theirs), own,
    )
    in_mine, in_theirs = call(
        input_kernel, [((n_pts, rows, enc), F32), ((n_pts, rows, enc), BF)],
        [
            pltpu.VMEM((points, enc), BF), pltpu.VMEM((points, hidden), BF),
            pltpu.VMEM((points, hidden), BF), pltpu.VMEM((hidden, width), BF),
            pltpu.VMEM((points, width), BF), dma((13,)),
        ],
        cost(5e10, 8e6), "shhhhhhha" + "vv", place, features, first, *mid, dz, own,
        mib=58,
    )
    strip = (maps // 2, width)
    grad_out, p_mine, p_theirs = call(
        functools.partial(sums_kernel, scale_b), [((rows, width), F32), (strip, F32), (strip, BF)],
        [], cost(1, 1), "svvvva" + "vvv",
        core_ref, exchange(s_code), wide_own, wide_other, w_out, in_mine,
    )
    part = p_mine + decode(swap_core(p_theirs))
    part = part.reshape(maps // 2, n_pts, width // n_pts).transpose(1, 0, 2)
    part = part.reshape(n_pts, rows, enc)

    wide_row = (rows, width)
    keep, *codes = call(
        fold_kernel, [(wide_row, F32)] + [(wide_row, BF)] * (n_hi - 1), [], cost(1, 1),
        "vv" + "v" * n_hi, own, move(low, 1),
    )
    (keep,) = call(hold_kernel, [(wide_row, F32)], [], cost(5e10, 1), "va" + "v", keep, codes[0])
    (last,) = call(
        pack_last_kernel, [((n_pts, rows, 2 * enc), BF)], [], cost(1, 1), "vvva" + "v",
        part, in_mine, swap_core(in_theirs), keep,
    )
    (keep,) = call(hold_kernel, [(wide_row, F32)], [], cost(5e10, 1), "va" + "v", keep, last)
    codes = [move(code, 2 * (k + 1)) for k, code in enumerate(codes)]
    (grad_mid,) = call(
        last_kernel, [(wide_row, F32)], [], cost(1, 1), "v" * n_hi + "v", keep, *codes
    )
    grad_branch, grad_in = call(
        last_small_kernel, [((rows, enc), F32), ((rows, enc), F32)],
        [], cost(1, 1), "v" + "vv", exchange(last),
    )
    grad_branch = grad_branch.reshape(maps // 2, width // n_pts).T
    return (grad_branch, grad_in, grad_mid, grad_out)


def solution(mesh):
    in_specs = (
        P(("grp", "pts", "maps"), None),
        P("maps", ("grp", "pts")),
        P(("grp", "maps"), "pts"),
        P(("pts", "maps"), None),
        P(("pts", "maps"), None),
        P(("pts", "maps"), None),
    )
    out_specs = (
        P("pts", ("grp", "maps")),
        P(("grp", "pts", "maps"), None),
        P(("grp", "pts", "maps"), None),
        P(("grp", "pts", "maps"), None),
    )
    return jax.shard_map(
        per_device, mesh=mesh, in_specs=in_specs, out_specs=out_specs, check_vma=False
    )
```

```python
import functools
import math

import jax
import jax.numpy as jnp
from jax import lax
from jax.experimental import pallas as pl
from jax.experimental.pallas import tpu as pltpu
from jax.sharding import PartitionSpec as P

BF = jnp.bfloat16
F32 = jnp.float32
MIB = 1024 * 1024
KERNEL_MIB = 12


def dot(left, right, left_dim, right_dim):
    return lax.dot_general(
        left, right, (((left_dim,), (right_dim,)), ((), ())), preferred_element_type=F32
    )


def split(value):
    high = value.astype(BF)
    return high, (value - high.astype(F32)).astype(BF)


def encode(value):
    return (value * value * value).astype(BF)


def decode(code):
    cube = code.astype(F32)
    size = jnp.abs(cube)
    root = jnp.exp2(jnp.log2(jnp.maximum(size, 1e-37)) * (1.0 / 3.0))
    return jnp.where(size < 1e-37, 0.0, jnp.where(cube < 0.0, -root, root))


def beside_kernel(*refs):
    *parts, out = refs
    at = 0
    for part in parts:
        out[:, at : at + part.shape[1]] = part[...]
        at += part.shape[1]


def stack_kernel(*refs):
    *parts, out = refs
    rows = parts[0].shape[0]
    for k, part in enumerate(parts):
        out[k * rows : (k + 1) * rows, :] = part[...]


def pair_kernel(own, got, out):
    rows = own.shape[0]
    out[:rows] = own[...]
    out[rows:] = got[...]


def both_kernel(core_ref, own, other, after, out):
    rows = own.shape[0]
    zero = core_ref[0] == 0
    a, b = own[...], other[...]
    out[:rows] = jnp.where(zero, a, b)
    out[rows:] = jnp.where(zero, b, a)


def fold_branch_kernel(scale_b, place_ref, w_both, *refs):
    *pairs, out, wide = refs
    if pairs[0].shape == wide.shape:
        wide[...] = pairs[0][...]
    else:
        maps = wide.shape[0]
        for k, pair in enumerate(pairs):
            each = pair.shape[1]
            for y in range(2):
                at = pl.multiple_of(place_ref[y * len(pairs) + k] * each, each)
                wide[:, pl.ds(at, each)] = pair[y * maps : (y + 1) * maps]
    code = encode(dot(wide[...], w_both[...], 1, 1) * scale_b)
    for p in range(out.shape[0]):
        out[p] = code


def main_kernel(
    scale_p, core_ref, features, near_a, near_b, far_a, far_b,
    b_own, b_other, target,
    far, near, s_mine, s_theirs, dz_out,
    first, second, dz, w_in, w_mid, pairs, b_all, branch, far_all, in_sem, out_sem,
):
    points, hidden = first.shape
    n_pts, rows, maps = s_mine.shape
    enc = features.shape[1]
    quarter, half, step = hidden // 4, hidden // 2, points // 4
    width = w_mid.shape[1]
    loads, loads_in = [], []
    for j, part in enumerate((near_a, near_b, far_a, far_b)):
        to = pl.ds(j * quarter, quarter)
        loads_in.append(
            pltpu.make_async_copy(part.at[:, pl.ds(width, enc)], w_in.at[to, :], in_sem.at[4 + j])
        )
        loads.append(
            pltpu.make_async_copy(part.at[:, pl.ds(0, width)], w_mid.at[to, :], in_sem.at[j])
        )
    for load in loads_in + loads:
        load.start()
    core = core_ref[0]
    for load in loads_in:
        load.wait()
    for i in range(4):
        block = slice(i * step, (i + 1) * step)
        first[block, :] = jnp.tanh(dot(features[block, :], w_in[...], 1, 1)).astype(BF)
    few = maps // 2
    for p in range(n_pts):
        cols = slice(2 * p * rows, 2 * (p + 1) * rows)
        branch[pl.ds(core * few, few), cols] = decode(b_own[p])
        branch[pl.ds((1 - core) * few, few), cols] = decode(b_other[p])
    bh, bl = split(branch[...])
    b_pair = jnp.concatenate([bh, bl], axis=0)
    b_three = jnp.concatenate([bh, bh, bl], axis=0)
    for load in loads:
        load.wait()
    for i in range(4):
        block = slice(i * step, (i + 1) * step)
        s = jnp.tanh(dot(first[block, :], w_mid[...], 1, 0)).astype(BF)
        second[block, :] = s
        pair = dot(s, b_pair, 1, 1)
        field = pair[:, :maps] + pair[:, maps:]
        resid = (field - target[block, :].astype(F32)) * scale_p
        rh, rl = split(resid)
        pairs[block, :] = jnp.concatenate([rh, rl], axis=1)
        s32 = s.astype(F32)
        back = dot(jnp.concatenate([rh, rl, rh], axis=1), b_three, 1, 0)
        dz[block, :] = (back * (1.0 - s32 * s32)).astype(BF)
    save_dz = pltpu.make_async_copy(dz, dz_out, out_sem.at[1])
    save_dz.start()
    both = dot(second[...], pairs[...], 0, 0)
    b_all[...] = both[:, :maps] + both[:, maps:]
    for p in range(n_pts):
        at = 2 * p * rows
        s_mine[p] = b_all[pl.ds(at + core * rows, rows), :]
        s_theirs[p] = encode(b_all[pl.ds(at + (1 - core) * rows, rows), :])
    saves = [save_dz]
    for i in range(4):
        block = slice(i * quarter, (i + 1) * quarter)
        g = dot(first[:, block], dz[...], 0, 0)
        if i < 2:
            near[block, :] = g
            continue
        part = slice((i - 2) * quarter, (i - 1) * quarter)
        far_all[part, :] = encode(g)
        saves.append(
            pltpu.make_async_copy(far_all.at[part, :], far.at[part, :], out_sem.at[i])
        )
        saves[-1].start()
    for save in saves:
        save.wait()


def send_kernel(near, got, low):
    quarter = low.shape[0]
    low[...] = encode(near[quarter:] + decode(got[quarter:]))


def keep_kernel(near, got, after, own):
    quarter = own.shape[0]
    own[...] = near[:quarter] + decode(got[:quarter])


def pack_sums_kernel(mine, got, after, out):
    out[...] = encode(mine[...] + decode(got[...]))


def sums_kernel(scale_b, core_ref, got, own, other, w_out, after, grad_out, mine, theirs):
    total = decode(got[0])
    for p in range(1, got.shape[0]):
        total += decode(got[p])
    sh, sl = split(total)
    w = w_out[...]
    zero = core_ref[0] == 0
    top, bottom = jnp.where(zero, own[...], other[...]), jnp.where(zero, other[...], own[...])
    b = jnp.concatenate([top, bottom], axis=0)
    grad_out[...] = (dot(sh, b, 1, 0) + dot(sl, b, 1, 0)) * scale_b
    part = (dot(sh, w, 0, 0) + dot(sl, w, 0, 0)) * scale_b
    half = part.shape[0] // 2
    mine[...] = jnp.where(zero, part[:half], part[half:])
    theirs[...] = encode(jnp.where(zero, part[half:], part[:half]))


def input_kernel(
    place_ref, features_in, near_a, near_b, far_a, far_b, dz_in, after, mine, theirs, done,
    features, grads, w_in, w_mid, dz, sem,
):
    points, hidden = grads.shape
    width, enc = dz.shape[1], features.shape[1]
    quarter, half, step = hidden // 4, hidden // 2, points // 4
    block = lambda i: slice(i * step, (i + 1) * step)
    load_features = pltpu.make_async_copy(features_in, features, sem.at[12])
    load_features.start()
    parts = (near_a, near_b, far_a, far_b)
    to = lambda j: pl.ds(j * quarter, quarter)
    small = [
        pltpu.make_async_copy(part.at[:, pl.ds(width, enc)], w_in.at[to(j), :], sem.at[4 + j])
        for j, part in enumerate(parts)
    ]
    large = [
        pltpu.make_async_copy(part.at[:, pl.ds(0, width)], w_mid.at[to(j), :], sem.at[j])
        for j, part in enumerate(parts)
    ]
    values = [
        pltpu.make_async_copy(dz_in.at[block(i), :], dz.at[block(i), :], sem.at[8 + i])
        for i in range(4)
    ]
    for load in (*small, values[0], *large, *values[1:]):
        load.start()
    load_features.wait()
    for load in small:
        load.wait()
    for i in range(4):
        f = jnp.tanh(dot(features[block(i), :], w_in[...], 1, 1)).astype(BF).astype(F32)
        slope = 1.0 - f * f
        values[i].wait()
        d = dz[block(i), :]
        for j in range(4):
            if i == 0:
                large[j].wait()
            cols = slice(j * quarter, (j + 1) * quarter)
            back = dot(d, w_mid[cols, :], 1, 1)
            grads[block(i), cols] = (back * slope[:, cols]).astype(BF)
    g = dot(features[...], grads[...], 0, 0).T
    done[...] = g[: done.shape[0]]
    n_pts, rows, _ = mine.shape
    for j in range(n_pts):
        p = place_ref[j]
        mine[p] = g[j * rows : (j + 1) * rows]
        theirs[p] = encode(g[half + j * rows : half + (j + 1) * rows])


def pack_last_kernel(part, mine, got, after, out):
    enc = part.shape[2]
    out[:, :, :enc] = encode(part[...])
    out[:, :, enc:] = encode(mine[...] + decode(got[...]))


def fold_kernel(own, got, keep, *codes):
    rows = keep.shape[0]
    keep[...] = own[:rows] + decode(got[:rows])
    for k, code in enumerate(codes):
        block = slice((k + 1) * rows, (k + 2) * rows)
        code[...] = encode(own[block] + decode(got[block]))


def hold_kernel(value, after, out):
    out[...] = value[...]


def last_kernel(keep, *refs):
    *codes, grad_mid = refs
    total = keep[...]
    for code in codes:
        total += decode(code[...])
    grad_mid[...] = total


def last_small_kernel(got, grad_branch, grad_in):
    total = decode(got[0])
    for p in range(1, got.shape[0]):
        total += decode(got[p])
    enc = grad_in.shape[1]
    grad_branch[...] = total[:, :enc]
    grad_in[...] = total[:, enc:]


def cost(flops, moved):
    return pl.CostEstimate(flops=int(flops), bytes_accessed=int(moved), transcendentals=0)


def call(kernel, outs, scratch, estimate, spaces, *args, mib=KERNEL_MIB):
    kinds = {"s": pltpu.SMEM, "v": pltpu.VMEM, "h": pltpu.HBM, "a": pl.ANY}
    specs = [pl.BlockSpec(memory_space=kinds[c]) for c in spaces]
    return pl.pallas_call(
        kernel,
        in_specs=specs[: len(args)],
        out_specs=specs[len(args) :],
        out_shape=[jax.ShapeDtypeStruct(shape, dtype) for shape, dtype in outs],
        scratch_shapes=scratch,
        compiler_params=pltpu.CompilerParams(vmem_limit_bytes=mib * MIB),
        cost_estimate=estimate,
    )(*args)


def per_device(features, target, branch, w_in, w_mid, w_out):
    n_pts = lax.axis_size("pts")
    core = lax.axis_index("maps")
    point = lax.axis_index("pts")
    rows, width = w_mid.shape
    hidden = rows * n_pts * 2
    quarter, half = hidden // 4, hidden // 2
    n_hi = n_pts // 2
    maps = 2 * branch.shape[0]
    points, enc = features.shape
    scale_b = 1.0 / math.sqrt(width)
    scale_p = 1.0 / math.sqrt(target.shape[1] * n_pts)
    swap_core = lambda v: lax.ppermute(v, "maps", [(0, 1), (1, 0)])
    move = lambda v, mask: lax.ppermute(v, "pts", [(i, i ^ mask) for i in range(n_pts)])
    exchange = lambda v: lax.all_to_all(v, "pts", 0, 0, tiled=True)
    pick = lambda flag, a, b: jnp.where(flag, a, b)
    first_core = core == 0
    core_ref = core.reshape(1)
    masks = [2 * k + y for y in range(2) for k in range(n_hi)]
    place = point ^ jnp.array(masks, jnp.int32)

    branch_own = branch.reshape(rows, enc)
    (pair,) = call(
        pair_kernel, [((2 * rows, enc), BF)], [], cost(1, 1), "vv" + "v",
        branch_own, move(branch_own, 1),
    )

    (own,) = call(
        beside_kernel, [((rows, width + enc), BF)], [], cost(1, 1), "vv" + "v", w_mid, w_in,
        mib=58,
    )
    (line,) = call(
        stack_kernel, [((quarter, width + enc), BF)], [], cost(1, 1e6), "v" * n_hi + "v",
        own, *[move(own, 2 * k) for k in range(1, n_hi)],
    )
    other = move(line, 1)
    mid = (line, other, swap_core(line), swap_core(other))

    square = width // n_pts == enc
    pairs = [pair] + [move(pair, 2 * k) for k in range(1, n_hi)]
    if not square:
        unmask = point ^ jnp.arange(n_pts, dtype=jnp.int32)
        small = jnp.stack(pairs).reshape(n_pts, *branch.shape)[unmask]
        pairs = [small.transpose(1, 0, 2).reshape(maps // 2, width)]
    (w_both,) = call(
        both_kernel, [((2 * rows, width), BF)], [], cost(5e10, 1), "svva" + "v",
        core_ref, w_out, swap_core(w_out), own,
    )
    folded, wide_own = call(
        functools.partial(fold_branch_kernel, scale_b),
        [((n_pts, maps // 2, 2 * rows), BF), ((maps // 2, width), BF)], [],
        cost(1, 1), "sv" + "v" * len(pairs) + "vv", place, w_both, *pairs,
    )
    b_own = exchange(folded)
    b_other = swap_core(b_own)
    wide_other = swap_core(wide_own)

    t_own = lax.dynamic_slice_in_dim(target, core * points, points, 1)
    t_other = swap_core(lax.dynamic_slice_in_dim(target, (1 - core) * points, points, 1))
    t_full = jnp.concatenate(
        [pick(first_core, t_own, t_other), pick(first_core, t_other, t_own)], axis=0
    ).T

    dma = pltpu.SemaphoreType.DMA
    far, near, s_mine, s_theirs, dz = call(
        functools.partial(main_kernel, scale_p),
        [((half, width), BF), ((half, width), F32), ((n_pts, rows, maps), F32)]
        + [((n_pts, rows, maps), BF), ((points, width), BF)],
        [
            pltpu.VMEM((points, hidden), BF), pltpu.VMEM((points, width), BF),
            pltpu.VMEM((points, width), BF), pltpu.VMEM((hidden, enc), BF),
            pltpu.VMEM((hidden, width), BF), pltpu.VMEM((points, 2 * maps), BF),
            pltpu.VMEM((width, maps), F32), pltpu.VMEM((maps, width), F32),
            pltpu.VMEM((half, width), BF), dma((8,)), dma((4,)),
        ],
        cost(5e10, 8e6), "svhhhhvvv" + "hvvvh",
        core_ref, features, *mid, b_own, b_other, t_full,
        mib=47,
    )

    far_got = swap_core(far)
    (low,) = call(
        send_kernel, [((quarter, width), BF)], [], cost(1, 1), "vv" + "v", near, far_got
    )
    (own,) = call(
        keep_kernel, [((quarter, width), F32)], [], cost(5e10, 1e6), "vva" + "v", near, far_got, low
    )

    (s_code,) = call(
        pack_sums_kernel, [((n_pts, rows, maps), BF)], [], cost(1, 1), "vva" + "v",
        s_mine, swap_core(s_theirs), own,
    )
    in_mine, in_theirs, in_done = call(
        input_kernel, [((n_pts, rows, enc), F32), ((n_pts, rows, enc), BF), ((8, enc), F32)],
        [
            pltpu.VMEM((points, enc), BF), pltpu.VMEM((points, hidden), BF),
            pltpu.VMEM((hidden, enc), BF), pltpu.VMEM((hidden, width), BF),
            pltpu.VMEM((points, width), BF), dma((13,)),
        ],
        cost(5e10, 8e6), "shhhhhha" + "vvv", place, features, *mid, dz, own,
        mib=54,
    )
    strip = (maps // 2, width)
    grad_out, p_mine, p_theirs = call(
        functools.partial(sums_kernel, scale_b), [((rows, width), F32), (strip, F32), (strip, BF)],
        [], cost(1, 1), "svvvva" + "vvv",
        core_ref, exchange(s_code), wide_own, wide_other, w_out, in_done,
    )
    part = p_mine + decode(swap_core(p_theirs))
    part = part.reshape(maps // 2, n_pts, width // n_pts).transpose(1, 0, 2)
    part = part.reshape(n_pts, rows, enc)

    wide_row = (rows, width)
    keep, *codes = call(
        fold_kernel, [(wide_row, F32)] + [(wide_row, BF)] * (n_hi - 1), [], cost(1, 1),
        "vv" + "v" * n_hi, own, move(low, 1),
    )
    (keep,) = call(hold_kernel, [(wide_row, F32)], [], cost(5e10, 1), "va" + "v", keep, codes[0])
    (last,) = call(
        pack_last_kernel, [((n_pts, rows, 2 * enc), BF)], [], cost(1, 1), "vvva" + "v",
        part, in_mine, swap_core(in_theirs), keep,
    )
    (keep,) = call(hold_kernel, [(wide_row, F32)], [], cost(5e10, 1), "va" + "v", keep, last)
    codes = [move(code, 2 * (k + 1)) for k, code in enumerate(codes)]
    (grad_mid,) = call(
        last_kernel, [(wide_row, F32)], [], cost(1, 1), "v" * n_hi + "v", keep, *codes
    )
    grad_branch, grad_in = call(
        last_small_kernel, [((rows, enc), F32), ((rows, enc), F32)],
        [], cost(1, 1), "v" + "vv", exchange(last),
    )
    grad_branch = grad_branch.reshape(maps // 2, width // n_pts).T
    return (grad_branch, grad_in, grad_mid, grad_out)


def solution(mesh):
    in_specs = (
        P(("grp", "pts", "maps"), None),
        P("maps", ("grp", "pts")),
        P(("grp", "maps"), "pts"),
        P(("pts", "maps"), None),
        P(("pts", "maps"), None),
        P(("pts", "maps"), None),
    )
    out_specs = (
        P("pts", ("grp", "maps")),
        P(("grp", "pts", "maps"), None),
        P(("grp", "pts", "maps"), None),
        P(("grp", "pts", "maps"), None),
    )
    return jax.shard_map(
        per_device, mesh=mesh, in_specs=in_specs, out_specs=out_specs, check_vma=False
    )
```

```python
import functools
import math

import jax
import jax.numpy as jnp
from jax import lax
from jax.experimental import pallas as pl
from jax.experimental.pallas import tpu as pltpu
from jax.sharding import PartitionSpec as P

BF = jnp.bfloat16
F32 = jnp.float32
MIB = 1024 * 1024
KERNEL_MIB = 12


def dot(left, right, left_dim, right_dim):
    return lax.dot_general(
        left, right, (((left_dim,), (right_dim,)), ((), ())), preferred_element_type=F32
    )


def split(value):
    high = value.astype(BF)
    return high, (value - high.astype(F32)).astype(BF)


def encode(value):
    return (value * value * value).astype(BF)


def decode(code):
    cube = code.astype(F32)
    size = jnp.abs(cube)
    root = jnp.exp2(jnp.log2(jnp.maximum(size, 1e-37)) * (1.0 / 3.0))
    return jnp.where(size < 1e-37, 0.0, jnp.where(cube < 0.0, -root, root))


def beside_kernel(*refs):
    *parts, out = refs
    at = 0
    for part in parts:
        out[:, at : at + part.shape[1]] = part[...]
        at += part.shape[1]


def stack_kernel(*refs):
    *parts, out = refs
    rows = parts[0].shape[0]
    for k, part in enumerate(parts):
        out[k * rows : (k + 1) * rows, :] = part[...]


def pair_kernel(own, got, out):
    rows = own.shape[0]
    out[:rows] = own[...]
    out[rows:] = got[...]


def both_kernel(core_ref, own, other, after, out):
    rows = own.shape[0]
    zero = core_ref[0] == 0
    a, b = own[...], other[...]
    out[:rows] = jnp.where(zero, a, b)
    out[rows:] = jnp.where(zero, b, a)


def fold_branch_kernel(scale_b, place_ref, w_both, *refs):
    *pairs, out, wide = refs
    if pairs[0].shape == wide.shape:
        wide[...] = pairs[0][...]
    else:
        maps = wide.shape[0]
        for k, pair in enumerate(pairs):
            each = pair.shape[1]
            for y in range(2):
                at = pl.multiple_of(place_ref[y * len(pairs) + k] * each, each)
                wide[:, pl.ds(at, each)] = pair[y * maps : (y + 1) * maps]
    code = encode(dot(wide[...], w_both[...], 1, 1) * scale_b)
    for p in range(out.shape[0]):
        out[p] = code


def main_kernel(
    scale_p, core_ref, features, near_a, near_b, far_a, far_b,
    b_own, b_other, target,
    far, near, s_mine, s_theirs, dz_out,
    first, second, dz, w_in, w_mid, pairs, branch, far_all, in_sem, out_sem,
):
    points, hidden = first.shape
    n_pts, few, rows = s_mine.shape
    rows, maps = rows // 2, 2 * few
    enc = features.shape[1]
    quarter, half, step = hidden // 4, hidden // 2, points // 4
    width = w_mid.shape[1]
    loads, loads_in = [], []
    for j, part in enumerate((near_a, near_b, far_a, far_b)):
        to = pl.ds(j * quarter, quarter)
        loads_in.append(
            pltpu.make_async_copy(part.at[:, pl.ds(width, enc)], w_in.at[to, :], in_sem.at[4 + j])
        )
        loads.append(
            pltpu.make_async_copy(part.at[:, pl.ds(0, width)], w_mid.at[to, :], in_sem.at[j])
        )
    for load in loads_in + loads:
        load.start()
    core = core_ref[0]
    for load in loads_in:
        load.wait()
    for i in range(4):
        block = slice(i * step, (i + 1) * step)
        first[block, :] = jnp.tanh(dot(features[block, :], w_in[...], 1, 1)).astype(BF)
    for p in range(n_pts):
        cols = slice(2 * p * rows, 2 * (p + 1) * rows)
        branch[pl.ds(core * few, few), cols] = decode(b_own[p])
        branch[pl.ds((1 - core) * few, few), cols] = decode(b_other[p])
    bh, bl = split(branch[...])
    b_pair = jnp.concatenate([bh, bl], axis=0)
    b_three = jnp.concatenate([bh, bh, bl], axis=0)
    for load in loads:
        load.wait()
    for i in range(4):
        block = slice(i * step, (i + 1) * step)
        s = jnp.tanh(dot(first[block, :], w_mid[...], 1, 0)).astype(BF)
        second[block, :] = s
        pair = dot(s, b_pair, 1, 1)
        field = pair[:, :maps] + pair[:, maps:]
        resid = (field - target[block, :].astype(F32)) * scale_p
        rh, rl = split(resid)
        pairs[block, :] = jnp.concatenate([rh, rl], axis=1)
        s32 = s.astype(F32)
        back = dot(jnp.concatenate([rh, rl, rh], axis=1), b_three, 1, 0)
        dz[block, :] = (back * (1.0 - s32 * s32)).astype(BF)
    save_dz = pltpu.make_async_copy(dz, dz_out, out_sem.at[1])
    save_dz.start()
    both = dot(pairs[...], second[...], 0, 0)
    sums = both[:maps] + both[maps:]
    zero = core == 0
    own, other = jnp.where(zero, sums[:few], sums[few:]), jnp.where(zero, sums[few:], sums[:few])
    for p in range(n_pts):
        cols = slice(2 * p * rows, 2 * (p + 1) * rows)
        s_mine[p] = own[:, cols]
        s_theirs[p] = encode(other[:, cols])
    saves = [save_dz]
    for i in range(4):
        block = slice(i * quarter, (i + 1) * quarter)
        g = dot(first[:, block], dz[...], 0, 0)
        if i < 2:
            near[block, :] = g
            continue
        part = slice((i - 2) * quarter, (i - 1) * quarter)
        far_all[part, :] = encode(g)
        saves.append(
            pltpu.make_async_copy(far_all.at[part, :], far.at[part, :], out_sem.at[i])
        )
        saves[-1].start()
    for save in saves:
        save.wait()


def send_kernel(near, got, low):
    quarter = low.shape[0]
    low[...] = encode(near[quarter:] + decode(got[quarter:]))


def keep_kernel(near, got, after, own):
    quarter = own.shape[0]
    own[...] = near[:quarter] + decode(got[:quarter])


def pack_sums_kernel(mine, got, after, out):
    out[...] = encode(mine[...] + decode(got[...]))


def sums_kernel(scale_b, got, w_both, after, total_out, part):
    total = decode(got[0])
    for p in range(1, got.shape[0]):
        total += decode(got[p])
    total_out[...] = total
    high, low = split(total)
    w = w_both[...]
    part[...] = (dot(high, w, 1, 0) + dot(low, w, 1, 0)) * scale_b


def grad_out_kernel(scale_b, core_ref, mine, theirs, own, other, after, grad_out):
    zero = core_ref[0] == 0
    rows = grad_out.shape[0]
    both = lambda a, b: jnp.concatenate(
        [jnp.where(zero, a[...], b[...]), jnp.where(zero, b[...], a[...])], axis=0
    )
    sums = both(mine, theirs)
    high, low = split(jnp.where(zero, sums[:, :rows], sums[:, rows:]))
    branch = both(own, other)
    grad_out[...] = (dot(high, branch, 0, 0) + dot(low, branch, 0, 0)) * scale_b


def input_kernel(
    place_ref, features_in, near_a, near_b, far_a, far_b, dz_in, after, mine, theirs, done,
    features, grads, w_in, w_mid, dz, sem,
):
    points, hidden = grads.shape
    width, enc = dz.shape[1], features.shape[1]
    quarter, half, step = hidden // 4, hidden // 2, points // 4
    block = lambda i: slice(i * step, (i + 1) * step)
    load_features = pltpu.make_async_copy(features_in, features, sem.at[12])
    load_features.start()
    parts = (near_a, near_b, far_a, far_b)
    to = lambda j: pl.ds(j * quarter, quarter)
    small = [
        pltpu.make_async_copy(part.at[:, pl.ds(width, enc)], w_in.at[to(j), :], sem.at[4 + j])
        for j, part in enumerate(parts)
    ]
    large = [
        pltpu.make_async_copy(part.at[:, pl.ds(0, width)], w_mid.at[to(j), :], sem.at[j])
        for j, part in enumerate(parts)
    ]
    values = [
        pltpu.make_async_copy(dz_in.at[block(i), :], dz.at[block(i), :], sem.at[8 + i])
        for i in range(4)
    ]
    for load in (*small, values[0], *large, *values[1:]):
        load.start()
    load_features.wait()
    for load in small:
        load.wait()
    for i in range(4):
        f = jnp.tanh(dot(features[block(i), :], w_in[...], 1, 1)).astype(BF).astype(F32)
        slope = 1.0 - f * f
        values[i].wait()
        d = dz[block(i), :]
        for j in range(4):
            if i == 0:
                large[j].wait()
            cols = slice(j * quarter, (j + 1) * quarter)
            back = dot(d, w_mid[cols, :], 1, 1)
            grads[block(i), cols] = (back * slope[:, cols]).astype(BF)
    g = dot(features[...], grads[...], 0, 0).T
    done[...] = g[: done.shape[0]]
    n_pts, rows, _ = mine.shape
    for j in range(n_pts):
        p = place_ref[j]
        mine[p] = g[j * rows : (j + 1) * rows]
        theirs[p] = encode(g[half + j * rows : half + (j + 1) * rows])


def pack_last_kernel(part, mine, got, after, out):
    enc = mine.shape[2]
    for p in range(out.shape[0]):
        block = part[p] if part.shape == mine.shape else part[:, p * enc : (p + 1) * enc]
        out[p, :, :enc] = encode(block)
    out[:, :, enc:] = encode(mine[...] + decode(got[...]))


def fold_kernel(own, got, keep, *codes):
    rows = keep.shape[0]
    keep[...] = own[:rows] + decode(got[:rows])
    for k, code in enumerate(codes):
        block = slice((k + 1) * rows, (k + 2) * rows)
        code[...] = encode(own[block] + decode(got[block]))


def hold_kernel(value, after, out):
    out[...] = value[...]


def last_kernel(keep, *refs):
    *codes, grad_mid = refs
    total = keep[...]
    for code in codes:
        total += decode(code[...])
    grad_mid[...] = total


def last_small_kernel(got, grad_branch, grad_in):
    total = decode(got[0])
    for p in range(1, got.shape[0]):
        total += decode(got[p])
    enc = grad_in.shape[1]
    grad_branch[...] = total[:, :enc]
    grad_in[...] = total[:, enc:]


def cost(flops, moved):
    return pl.CostEstimate(flops=int(flops), bytes_accessed=int(moved), transcendentals=0)


def call(kernel, outs, scratch, estimate, spaces, *args, mib=KERNEL_MIB):
    kinds = {"s": pltpu.SMEM, "v": pltpu.VMEM, "h": pltpu.HBM, "a": pl.ANY}
    specs = [pl.BlockSpec(memory_space=kinds[c]) for c in spaces]
    return pl.pallas_call(
        kernel,
        in_specs=specs[: len(args)],
        out_specs=specs[len(args) :],
        out_shape=[jax.ShapeDtypeStruct(shape, dtype) for shape, dtype in outs],
        scratch_shapes=scratch,
        compiler_params=pltpu.CompilerParams(vmem_limit_bytes=mib * MIB),
        cost_estimate=estimate,
    )(*args)


def per_device(features, target, branch, w_in, w_mid, w_out):
    n_pts = lax.axis_size("pts")
    core = lax.axis_index("maps")
    point = lax.axis_index("pts")
    rows, width = w_mid.shape
    hidden = rows * n_pts * 2
    quarter, half = hidden // 4, hidden // 2
    n_hi = n_pts // 2
    maps = 2 * branch.shape[0]
    points, enc = features.shape
    scale_b = 1.0 / math.sqrt(width)
    scale_p = 1.0 / math.sqrt(target.shape[1] * n_pts)
    swap_core = lambda v: lax.ppermute(v, "maps", [(0, 1), (1, 0)])
    move = lambda v, mask: lax.ppermute(v, "pts", [(i, i ^ mask) for i in range(n_pts)])
    exchange = lambda v: lax.all_to_all(v, "pts", 0, 0, tiled=True)
    pick = lambda flag, a, b: jnp.where(flag, a, b)
    first_core = core == 0
    core_ref = core.reshape(1)
    masks = [2 * k + y for y in range(2) for k in range(n_hi)]
    place = point ^ jnp.array(masks, jnp.int32)

    branch_own = branch.reshape(rows, enc)
    (pair,) = call(
        pair_kernel, [((2 * rows, enc), BF)], [], cost(1, 1), "vv" + "v",
        branch_own, move(branch_own, 1),
    )

    (own,) = call(
        beside_kernel, [((rows, width + enc), BF)], [], cost(1, 1), "vv" + "v", w_mid, w_in,
        mib=58,
    )
    (line,) = call(
        stack_kernel, [((quarter, width + enc), BF)], [], cost(1, 1e6), "v" * n_hi + "v",
        own, *[move(own, 2 * k) for k in range(1, n_hi)],
    )
    other = move(line, 1)
    mid = (line, other, swap_core(line), swap_core(other))

    square = width // n_pts == enc
    pairs = [pair] + [move(pair, 2 * k) for k in range(1, n_hi)]
    if not square:
        unmask = point ^ jnp.arange(n_pts, dtype=jnp.int32)
        small = jnp.stack(pairs).reshape(n_pts, *branch.shape)[unmask]
        pairs = [small.transpose(1, 0, 2).reshape(maps // 2, width)]
    (w_both,) = call(
        both_kernel, [((2 * rows, width), BF)], [], cost(5e10, 1), "svva" + "v",
        core_ref, w_out, swap_core(w_out), own,
    )
    folded, wide_own = call(
        functools.partial(fold_branch_kernel, scale_b),
        [((n_pts, maps // 2, 2 * rows), BF), ((maps // 2, width), BF)], [],
        cost(1, 1), "sv" + "v" * len(pairs) + "vv", place, w_both, *pairs,
    )
    b_own = exchange(folded)
    b_other = swap_core(b_own)
    wide_other = swap_core(wide_own)

    t_own = lax.dynamic_slice_in_dim(target, core * points, points, 1)
    t_other = swap_core(lax.dynamic_slice_in_dim(target, (1 - core) * points, points, 1))
    t_full = jnp.concatenate(
        [pick(first_core, t_own, t_other), pick(first_core, t_other, t_own)], axis=0
    ).T

    dma = pltpu.SemaphoreType.DMA
    sums_block = (n_pts, maps // 2, 2 * rows)
    far, near, s_mine, s_theirs, dz = call(
        functools.partial(main_kernel, scale_p),
        [((half, width), BF), ((half, width), F32), (sums_block, F32), (sums_block, BF)]
        + [((points, width), BF)],
        [
            pltpu.VMEM((points, hidden), BF), pltpu.VMEM((points, width), BF),
            pltpu.VMEM((points, width), BF), pltpu.VMEM((hidden, enc), BF),
            pltpu.VMEM((hidden, width), BF), pltpu.VMEM((points, 2 * maps), BF),
            pltpu.VMEM((maps, width), F32),
            pltpu.VMEM((half, width), BF), dma((8,)), dma((4,)),
        ],
        cost(5e10, 8e6), "svhhhhvvv" + "hvvvh",
        core_ref, features, *mid, b_own, b_other, t_full,
        mib=47,
    )

    far_got = swap_core(far)
    (low,) = call(
        send_kernel, [((quarter, width), BF)], [], cost(1, 1), "vv" + "v", near, far_got
    )
    (own,) = call(
        keep_kernel, [((quarter, width), F32)], [], cost(5e10, 1e6), "vva" + "v", near, far_got, low
    )

    (s_code,) = call(
        pack_sums_kernel, [(sums_block, BF)], [], cost(1, 1), "vva" + "v",
        s_mine, swap_core(s_theirs), own,
    )
    in_mine, in_theirs, in_done = call(
        input_kernel, [((n_pts, rows, enc), F32), ((n_pts, rows, enc), BF), ((8, enc), F32)],
        [
            pltpu.VMEM((points, enc), BF), pltpu.VMEM((points, hidden), BF),
            pltpu.VMEM((hidden, enc), BF), pltpu.VMEM((hidden, width), BF),
            pltpu.VMEM((points, width), BF), dma((13,)),
        ],
        cost(5e10, 8e6), "shhhhhha" + "vvv", place, features, *mid, dz, own,
        mib=54,
    )
    total, part = call(
        functools.partial(sums_kernel, scale_b),
        [((maps // 2, 2 * rows), F32), ((maps // 2, width), F32)],
        [], cost(1, 1), "vva" + "vv", exchange(s_code), w_both, in_done,
    )
    if not square:
        part = part.reshape(maps // 2, n_pts, width // n_pts).transpose(1, 0, 2)
        part = part.reshape(n_pts, rows, enc)

    wide_row = (rows, width)
    keep, *codes = call(
        fold_kernel, [(wide_row, F32)] + [(wide_row, BF)] * (n_hi - 1), [], cost(1, 1),
        "vv" + "v" * n_hi, own, move(low, 1),
    )
    (keep,) = call(hold_kernel, [(wide_row, F32)], [], cost(5e10, 1), "va" + "v", keep, codes[0])
    (last,) = call(
        pack_last_kernel, [((n_pts, rows, 2 * enc), BF)], [], cost(1, 1), "vvva" + "v",
        part, in_mine, swap_core(in_theirs), keep,
    )
    (keep,) = call(hold_kernel, [(wide_row, F32)], [], cost(5e10, 1), "va" + "v", keep, last)
    (grad_out,) = call(
        functools.partial(grad_out_kernel, scale_b), [((rows, width), F32)], [], cost(1, 1),
        "svvvva" + "v", core_ref, total, swap_core(total), wide_own, wide_other, keep,
    )
    codes = [move(code, 2 * (k + 1)) for k, code in enumerate(codes)]
    (grad_mid,) = call(
        last_kernel, [(wide_row, F32)], [], cost(1, 1), "v" * n_hi + "v", keep, *codes
    )
    grad_branch, grad_in = call(
        last_small_kernel, [((rows, enc), F32), ((rows, enc), F32)],
        [], cost(1, 1), "v" + "vv", exchange(last),
    )
    grad_branch = grad_branch.reshape(maps // 2, width // n_pts).T
    return (grad_branch, grad_in, grad_mid, grad_out)


def solution(mesh):
    in_specs = (
        P(("grp", "pts", "maps"), None),
        P("maps", ("grp", "pts")),
        P(("grp", "maps"), "pts"),
        P(("pts", "maps"), None),
        P(("pts", "maps"), None),
        P(("pts", "maps"), None),
    )
    out_specs = (
        P("pts", ("grp", "maps")),
        P(("grp", "pts", "maps"), None),
        P(("grp", "pts", "maps"), None),
        P(("grp", "pts", "maps"), None),
    )
    return jax.shard_map(
        per_device, mesh=mesh, in_specs=in_specs, out_specs=out_specs, check_vma=False
    )
```

```python
import functools
import math

import jax
import jax.numpy as jnp
from jax import lax
from jax.experimental import pallas as pl
from jax.experimental.pallas import tpu as pltpu
from jax.sharding import PartitionSpec as P

BF = jnp.bfloat16
F32 = jnp.float32
MIB = 1024 * 1024
KERNEL_MIB = 12


def dot(left, right, left_dim, right_dim):
    return lax.dot_general(
        left, right, (((left_dim,), (right_dim,)), ((), ())), preferred_element_type=F32
    )


def split(value):
    high = value.astype(BF)
    return high, (value - high.astype(F32)).astype(BF)


def encode(value):
    return (value * value * value).astype(BF)


def decode(code):
    cube = code.astype(F32)
    size = jnp.abs(cube)
    root = jnp.exp2(jnp.log2(jnp.maximum(size, 1e-37)) * (1.0 / 3.0))
    return jnp.where(size < 1e-37, 0.0, jnp.where(cube < 0.0, -root, root))


def beside_kernel(*refs):
    *parts, out = refs
    at = 0
    for part in parts:
        out[:, at : at + part.shape[1]] = part[...]
        at += part.shape[1]


def stack_kernel(*refs):
    *parts, out = refs
    rows = parts[0].shape[0]
    for k, part in enumerate(parts):
        out[k * rows : (k + 1) * rows, :] = part[...]


def pair_kernel(own, got, out):
    rows = own.shape[0]
    out[:rows] = own[...]
    out[rows:] = got[...]


def both_kernel(core_ref, own, other, after, out):
    rows = own.shape[0]
    zero = core_ref[0] == 0
    a, b = own[...], other[...]
    out[:rows] = jnp.where(zero, a, b)
    out[rows:] = jnp.where(zero, b, a)


def fold_branch_kernel(scale_b, place_ref, w_both, *refs):
    *pairs, out, wide = refs
    if pairs[0].shape == wide.shape:
        wide[...] = pairs[0][...]
    else:
        maps = wide.shape[0]
        for k, pair in enumerate(pairs):
            each = pair.shape[1]
            for y in range(2):
                at = pl.multiple_of(place_ref[y * len(pairs) + k] * each, each)
                wide[:, pl.ds(at, each)] = pair[y * maps : (y + 1) * maps]
    code = encode(dot(wide[...], w_both[...], 1, 1) * scale_b)
    for p in range(out.shape[0]):
        out[p] = code


def main_kernel(
    scale_p, core_ref, features, near_a, near_b, far_a, far_b,
    b_own, b_other, target,
    far, near, s_mine, s_theirs, dz_out,
    first, second, dz, w_in, w_mid, pairs, branch, far_all, in_sem, out_sem,
):
    points, hidden = first.shape
    n_pts, few, rows = s_mine.shape
    rows, maps = rows // 2, 2 * few
    enc = features.shape[1]
    quarter, half, step = hidden // 4, hidden // 2, points // 4
    width = w_mid.shape[1]
    loads, loads_in = [], []
    for j, part in enumerate((near_a, near_b, far_a, far_b)):
        to = pl.ds(j * quarter, quarter)
        loads_in.append(
            pltpu.make_async_copy(part.at[:, pl.ds(width, enc)], w_in.at[to, :], in_sem.at[4 + j])
        )
        loads.append(
            pltpu.make_async_copy(part.at[:, pl.ds(0, width)], w_mid.at[to, :], in_sem.at[j])
        )
    for load in loads_in + loads:
        load.start()
    core = core_ref[0]
    for load in loads_in:
        load.wait()
    for i in range(4):
        block = slice(i * step, (i + 1) * step)
        first[block, :] = jnp.tanh(dot(features[block, :], w_in[...], 1, 1)).astype(BF)
    for p in range(n_pts):
        cols = slice(2 * p * rows, 2 * (p + 1) * rows)
        branch[pl.ds(core * few, few), cols] = decode(b_own[p])
        branch[pl.ds((1 - core) * few, few), cols] = decode(b_other[p])
    bh, bl = split(branch[...])
    b_pair = jnp.concatenate([bh, bl], axis=0)
    b_three = jnp.concatenate([bh, bh, bl], axis=0)
    for load in loads:
        load.wait()
    for i in range(4):
        block = slice(i * step, (i + 1) * step)
        s = jnp.tanh(dot(first[block, :], w_mid[...], 1, 0)).astype(BF)
        second[block, :] = s
        pair = dot(s, b_pair, 1, 1)
        field = pair[:, :maps] + pair[:, maps:]
        resid = (field - target[block, :].astype(F32)) * scale_p
        rh, rl = split(resid)
        pairs[block, :] = jnp.concatenate([rh, rl], axis=1)
        s32 = s.astype(F32)
        back = dot(jnp.concatenate([rh, rl, rh], axis=1), b_three, 1, 0)
        dz[block, :] = (back * (1.0 - s32 * s32)).astype(BF)
    save_dz = pltpu.make_async_copy(dz, dz_out, out_sem.at[1])
    save_dz.start()
    both = dot(pairs[...], second[...], 0, 0)
    sums = both[:maps] + both[maps:]
    zero = core == 0
    own, other = jnp.where(zero, sums[:few], sums[few:]), jnp.where(zero, sums[few:], sums[:few])
    for p in range(n_pts):
        cols = slice(2 * p * rows, 2 * (p + 1) * rows)
        s_mine[p] = own[:, cols]
        s_theirs[p] = encode(other[:, cols])
    saves = [save_dz]
    for i in range(4):
        block = slice(i * quarter, (i + 1) * quarter)
        g = dot(first[:, block], dz[...], 0, 0)
        if i < 2:
            near[block, :] = g
            continue
        part = slice((i - 2) * quarter, (i - 1) * quarter)
        far_all[part, :] = encode(g)
        saves.append(
            pltpu.make_async_copy(far_all.at[part, :], far.at[part, :], out_sem.at[i])
        )
        saves[-1].start()
    for save in saves:
        save.wait()


def send_kernel(near, got, low):
    quarter = low.shape[0]
    low[...] = encode(near[quarter:] + decode(got[quarter:]))


def keep_kernel(near, got, after, own):
    quarter = own.shape[0]
    own[...] = near[:quarter] + decode(got[:quarter])


def pack_sums_kernel(mine, got, after, out):
    out[...] = encode(mine[...] + decode(got[...]))


def sums_kernel(scale_b, got, w_both, after, total_out, part):
    total = decode(got[0])
    for p in range(1, got.shape[0]):
        total += decode(got[p])
    total_out[...] = total
    high, low = split(total)
    w = w_both[...]
    part[...] = (dot(high, w, 1, 0) + dot(low, w, 1, 0)) * scale_b


def grad_out_kernel(scale_b, core_ref, mine, theirs, own, other, after, grad_out):
    zero = core_ref[0] == 0
    rows = grad_out.shape[0]
    both = lambda a, b: jnp.concatenate(
        [jnp.where(zero, a[...], b[...]), jnp.where(zero, b[...], a[...])], axis=0
    )
    sums = both(mine, theirs)
    high, low = split(jnp.where(zero, sums[:, :rows], sums[:, rows:]))
    branch = both(own, other)
    grad_out[...] = (dot(high, branch, 0, 0) + dot(low, branch, 0, 0)) * scale_b


def input_kernel(
    place_ref, features_in, near_a, near_b, far_a, far_b, dz_in, after, mine, theirs, done,
    features, grads, w_in, w_mid, dz, sem,
):
    points, hidden = grads.shape
    width, enc = dz.shape[1], features.shape[1]
    quarter, half, step = hidden // 4, hidden // 2, points // 4
    block = lambda i: slice(i * step, (i + 1) * step)
    load_features = pltpu.make_async_copy(features_in, features, sem.at[12])
    load_features.start()
    parts = (near_a, near_b, far_a, far_b)
    to = lambda j: pl.ds(j * quarter, quarter)
    small = [
        pltpu.make_async_copy(part.at[:, pl.ds(width, enc)], w_in.at[to(j), :], sem.at[4 + j])
        for j, part in enumerate(parts)
    ]
    large = [
        pltpu.make_async_copy(part.at[:, pl.ds(0, width)], w_mid.at[to(j), :], sem.at[j])
        for j, part in enumerate(parts)
    ]
    values = [
        pltpu.make_async_copy(dz_in.at[block(i), :], dz.at[block(i), :], sem.at[8 + i])
        for i in range(4)
    ]
    for load in (*small, values[0], *large, *values[1:]):
        load.start()
    load_features.wait()
    for load in small:
        load.wait()
    for i in range(4):
        f = jnp.tanh(dot(features[block(i), :], w_in[...], 1, 1)).astype(BF).astype(F32)
        slope = 1.0 - f * f
        values[i].wait()
        d = dz[block(i), :]
        for j in range(4):
            if i == 0:
                large[j].wait()
            cols = slice(j * quarter, (j + 1) * quarter)
            back = dot(d, w_mid[cols, :], 1, 1)
            grads[block(i), cols] = (back * slope[:, cols]).astype(BF)
    g = dot(features[...], grads[...], 0, 0).T
    done[...] = g[: done.shape[0]]
    n_pts, rows, _ = mine.shape
    for j in range(n_pts):
        p = place_ref[j]
        mine[p] = g[j * rows : (j + 1) * rows]
        theirs[p] = encode(g[half + j * rows : half + (j + 1) * rows])


def pack_last_kernel(part, mine, got, after, out):
    enc = mine.shape[2]
    for p in range(out.shape[0]):
        block = part[p] if part.shape == mine.shape else part[:, p * enc : (p + 1) * enc]
        out[p, :, :enc] = encode(block)
    out[:, :, enc:] = encode(mine[...] + decode(got[...]))


def fold_kernel(own, got, keep, *codes):
    rows = keep.shape[0]
    keep[...] = own[:rows] + decode(got[:rows])
    for k, code in enumerate(codes):
        block = slice((k + 1) * rows, (k + 2) * rows)
        code[...] = encode(own[block] + decode(got[block]))


def hold_kernel(value, after, out):
    out[...] = value[...]


def last_kernel(keep, *refs):
    *codes, grad_mid = refs
    total = keep[...]
    for code in codes:
        total += decode(code[...])
    grad_mid[...] = total


def last_small_kernel(got, grad_branch, grad_in):
    total = decode(got[0])
    for p in range(1, got.shape[0]):
        total += decode(got[p])
    enc = grad_in.shape[1]
    grad_branch[...] = total[:, :enc]
    grad_in[...] = total[:, enc:]


def cost(flops, moved):
    return pl.CostEstimate(flops=int(flops), bytes_accessed=int(moved), transcendentals=0)


def call(kernel, outs, scratch, estimate, spaces, *args, mib=KERNEL_MIB):
    kinds = {"s": pltpu.SMEM, "v": pltpu.VMEM, "h": pltpu.HBM, "a": pl.ANY}
    specs = [pl.BlockSpec(memory_space=kinds[c]) for c in spaces]
    return pl.pallas_call(
        kernel,
        in_specs=specs[: len(args)],
        out_specs=specs[len(args) :],
        out_shape=[jax.ShapeDtypeStruct(shape, dtype) for shape, dtype in outs],
        scratch_shapes=scratch,
        compiler_params=pltpu.CompilerParams(vmem_limit_bytes=mib * MIB),
        cost_estimate=estimate,
    )(*args)


def per_device(features, target, branch, w_in, w_mid, w_out):
    n_pts = lax.axis_size("pts")
    core = lax.axis_index("maps")
    point = lax.axis_index("pts")
    rows, width = w_mid.shape
    hidden = rows * n_pts * 2
    quarter, half = hidden // 4, hidden // 2
    n_hi = n_pts // 2
    maps = 2 * branch.shape[0]
    points, enc = features.shape
    scale_b = 1.0 / math.sqrt(width)
    scale_p = 1.0 / math.sqrt(target.shape[1] * n_pts)
    swap_core = lambda v: lax.ppermute(v, "maps", [(0, 1), (1, 0)])
    move = lambda v, mask: lax.ppermute(v, "pts", [(i, i ^ mask) for i in range(n_pts)])
    exchange = lambda v: lax.all_to_all(v, "pts", 0, 0, tiled=True)
    pick = lambda flag, a, b: jnp.where(flag, a, b)
    first_core = core == 0
    core_ref = core.reshape(1)
    masks = [2 * k + y for y in range(2) for k in range(n_hi)]
    place = point ^ jnp.array(masks, jnp.int32)

    branch_own = branch.reshape(rows, enc)
    (pair,) = call(
        pair_kernel, [((2 * rows, enc), BF)], [], cost(1, 1), "vv" + "v",
        branch_own, move(branch_own, 1),
    )

    (own,) = call(
        beside_kernel, [((rows, width + enc), BF)], [], cost(1, 1), "vv" + "v", w_mid, w_in,
        mib=58,
    )
    (line,) = call(
        stack_kernel, [((quarter, width + enc), BF)], [], cost(1, 1e6), "v" * n_hi + "v",
        own, *[move(own, 2 * k) for k in range(1, n_hi)],
    )
    other = move(line, 1)
    mid = (line, other, swap_core(line), swap_core(other))

    square = width // n_pts == enc
    pairs = [pair] + [move(pair, 2 * k) for k in range(1, n_hi)]
    if not square:
        unmask = point ^ jnp.arange(n_pts, dtype=jnp.int32)
        small = jnp.stack(pairs).reshape(n_pts, *branch.shape)[unmask]
        pairs = [small.transpose(1, 0, 2).reshape(maps // 2, width)]
    (w_both,) = call(
        both_kernel, [((2 * rows, width), BF)], [], cost(5e10, 1), "svva" + "v",
        core_ref, w_out, swap_core(w_out), own,
    )
    folded, wide_own = call(
        functools.partial(fold_branch_kernel, scale_b),
        [((n_pts, maps // 2, 2 * rows), BF), ((maps // 2, width), BF)], [],
        cost(1, 1), "sv" + "v" * len(pairs) + "vv", place, w_both, *pairs,
    )
    b_own = exchange(folded)
    b_other = swap_core(b_own)
    wide_other = swap_core(wide_own)

    t_own = lax.dynamic_slice_in_dim(target, core * points, points, 1)
    t_other = swap_core(lax.dynamic_slice_in_dim(target, (1 - core) * points, points, 1))
    t_full = jnp.concatenate(
        [pick(first_core, t_own, t_other), pick(first_core, t_other, t_own)], axis=0
    ).T

    dma = pltpu.SemaphoreType.DMA
    sums_block = (n_pts, maps // 2, 2 * rows)
    far, near, s_mine, s_theirs, dz = call(
        functools.partial(main_kernel, scale_p),
        [((half, width), BF), ((half, width), F32), (sums_block, F32), (sums_block, BF)]
        + [((points, width), BF)],
        [
            pltpu.VMEM((points, hidden), BF), pltpu.VMEM((points, width), BF),
            pltpu.VMEM((points, width), BF), pltpu.VMEM((hidden, enc), BF),
            pltpu.VMEM((hidden, width), BF), pltpu.VMEM((points, 2 * maps), BF),
            pltpu.VMEM((maps, width), F32),
            pltpu.VMEM((half, width), BF), dma((8,)), dma((4,)),
        ],
        cost(5e10, 8e6), "svhhhhvvv" + "hvvvh",
        core_ref, features, *mid, b_own, b_other, t_full,
        mib=47,
    )

    far_got = swap_core(far)
    (low,) = call(
        send_kernel, [((quarter, width), BF)], [], cost(1, 1), "vv" + "v", near, far_got
    )
    (own,) = call(
        keep_kernel, [((quarter, width), F32)], [], cost(5e10, 1e6), "vva" + "v", near, far_got, low
    )

    (s_code,) = call(
        pack_sums_kernel, [(sums_block, BF)], [], cost(1, 1), "vva" + "v",
        s_mine, swap_core(s_theirs), own,
    )
    in_mine, in_theirs, in_done = call(
        input_kernel, [((n_pts, rows, enc), F32), ((n_pts, rows, enc), BF), ((8, enc), F32)],
        [
            pltpu.VMEM((points, enc), BF), pltpu.VMEM((points, hidden), BF),
            pltpu.VMEM((hidden, enc), BF), pltpu.VMEM((hidden, width), BF),
            pltpu.VMEM((points, width), BF), dma((13,)),
        ],
        cost(5e10, 8e6), "shhhhhha" + "vvv", place, features, *mid, dz, own,
        mib=54,
    )
    total, part = call(
        functools.partial(sums_kernel, scale_b),
        [((maps // 2, 2 * rows), F32), ((maps // 2, width), F32)],
        [], cost(1, 1), "vva" + "vv", exchange(s_code), w_both, in_done,
    )
    if not square:
        part = part.reshape(maps // 2, n_pts, width // n_pts).transpose(1, 0, 2)
        part = part.reshape(n_pts, rows, enc)

    wide_row = (rows, width)
    keep, *codes = call(
        fold_kernel, [(wide_row, F32)] + [(wide_row, BF)] * (n_hi - 1), [], cost(1, 1),
        "vv" + "v" * n_hi, own, move(low, 1),
    )
    (keep,) = call(hold_kernel, [(wide_row, F32)], [], cost(5e10, 1), "va" + "v", keep, codes[0])
    (last,) = call(
        pack_last_kernel, [((n_pts, rows, 2 * enc), BF)], [], cost(1, 1), "vvva" + "v",
        part, in_mine, swap_core(in_theirs), keep,
    )
    (keep,) = call(hold_kernel, [(wide_row, F32)], [], cost(5e10, 1), "va" + "v", keep, last)
    (grad_out,) = call(
        functools.partial(grad_out_kernel, scale_b), [((rows, width), F32)], [], cost(1, 1),
        "svvvva" + "v", core_ref, total, swap_core(total), wide_own, wide_other, keep,
    )
    codes = [move(codes[k], 2 * (k + 1)) for k in reversed(range(len(codes)))]
    (grad_mid,) = call(
        last_kernel, [(wide_row, F32)], [], cost(1, 1), "v" * n_hi + "v", keep, *codes
    )
    grad_branch, grad_in = call(
        last_small_kernel, [((rows, enc), F32), ((rows, enc), F32)],
        [], cost(1, 1), "v" + "vv", exchange(last),
    )
    grad_branch = grad_branch.reshape(maps // 2, width // n_pts).T
    return (grad_branch, grad_in, grad_mid, grad_out)


def solution(mesh):
    in_specs = (
        P(("grp", "pts", "maps"), None),
        P("maps", ("grp", "pts")),
        P(("grp", "maps"), "pts"),
        P(("pts", "maps"), None),
        P(("pts", "maps"), None),
        P(("pts", "maps"), None),
    )
    out_specs = (
        P("pts", ("grp", "maps")),
        P(("grp", "pts", "maps"), None),
        P(("grp", "pts", "maps"), None),
        P(("grp", "pts", "maps"), None),
    )
    return jax.shard_map(
        per_device, mesh=mesh, in_specs=in_specs, out_specs=out_specs, check_vma=False
    )
```

```python
import functools
import math

import jax
import jax.numpy as jnp
from jax import lax
from jax.experimental import pallas as pl
from jax.experimental.pallas import tpu as pltpu
from jax.sharding import PartitionSpec as P

BF = jnp.bfloat16
F32 = jnp.float32
MIB = 1024 * 1024
KERNEL_MIB = 12


def dot(left, right, left_dim, right_dim):
    return lax.dot_general(
        left, right, (((left_dim,), (right_dim,)), ((), ())), preferred_element_type=F32
    )


def split(value):
    high = value.astype(BF)
    return high, (value - high.astype(F32)).astype(BF)


def encode(value):
    return (value * value * value).astype(BF)


def decode(code):
    cube = code.astype(F32)
    size = jnp.abs(cube)
    root = jnp.exp2(jnp.log2(jnp.maximum(size, 1e-37)) * (1.0 / 3.0))
    return jnp.where(size < 1e-37, 0.0, jnp.where(cube < 0.0, -root, root))


def beside_kernel(*refs):
    *parts, out = refs
    at = 0
    for part in parts:
        out[:, at : at + part.shape[1]] = part[...]
        at += part.shape[1]


def stack_kernel(*refs):
    *parts, out = refs
    rows = parts[0].shape[0]
    for k, part in enumerate(parts):
        out[k * rows : (k + 1) * rows, :] = part[...]


def pair_kernel(own, got, out):
    rows = own.shape[0]
    out[:rows] = own[...]
    out[rows:] = got[...]


def both_kernel(core_ref, own, other, after, out):
    rows = own.shape[0]
    zero = core_ref[0] == 0
    a, b = own[...], other[...]
    out[:rows] = jnp.where(zero, a, b)
    out[rows:] = jnp.where(zero, b, a)


def fold_branch_kernel(scale_b, place_ref, w_both, *refs):
    *pairs, out, wide = refs
    if pairs[0].shape == wide.shape:
        wide[...] = pairs[0][...]
    else:
        maps = wide.shape[0]
        for k, pair in enumerate(pairs):
            each = pair.shape[1]
            for y in range(2):
                at = pl.multiple_of(place_ref[y * len(pairs) + k] * each, each)
                wide[:, pl.ds(at, each)] = pair[y * maps : (y + 1) * maps]
    code = encode(dot(wide[...], w_both[...], 1, 1) * scale_b)
    for p in range(out.shape[0]):
        out[p] = code


def main_kernel(
    scale_p, core_ref, features, near_a, near_b, far_a, far_b,
    b_own, b_other, target,
    far, near, s_mine, s_theirs, dz_out,
    first, second, dz, w_in, w_mid, pairs, branch, far_all, in_sem, out_sem,
):
    points, hidden = first.shape
    n_pts, few, rows = s_mine.shape
    rows, maps = rows // 2, 2 * few
    enc = features.shape[1]
    quarter, half, step = hidden // 4, hidden // 2, points // 4
    width = w_mid.shape[1]
    loads, loads_in = [], []
    for j, part in enumerate((near_a, near_b, far_a, far_b)):
        to = pl.ds(j * quarter, quarter)
        loads_in.append(
            pltpu.make_async_copy(part.at[:, pl.ds(width, enc)], w_in.at[to, :], in_sem.at[4 + j])
        )
        loads.append(
            pltpu.make_async_copy(part.at[:, pl.ds(0, width)], w_mid.at[to, :], in_sem.at[j])
        )
    for load in loads_in + loads:
        load.start()
    core = core_ref[0]
    for load in loads_in:
        load.wait()
    for i in range(4):
        block = slice(i * step, (i + 1) * step)
        first[block, :] = jnp.tanh(dot(features[block, :], w_in[...], 1, 1)).astype(BF)
    for p in range(n_pts):
        cols = slice(2 * p * rows, 2 * (p + 1) * rows)
        branch[pl.ds(core * few, few), cols] = decode(b_own[p])
        branch[pl.ds((1 - core) * few, few), cols] = decode(b_other[p])
    bh, bl = split(branch[...])
    b_pair = jnp.concatenate([bh, bl], axis=0)
    b_three = jnp.concatenate([bh, bh, bl], axis=0)
    for load in loads:
        load.wait()
    for i in range(4):
        block = slice(i * step, (i + 1) * step)
        s = jnp.tanh(dot(first[block, :], w_mid[...], 1, 0)).astype(BF)
        second[block, :] = s
        pair = dot(s, b_pair, 1, 1)
        field = pair[:, :maps] + pair[:, maps:]
        resid = (field - target[block, :].astype(F32)) * scale_p
        rh, rl = split(resid)
        pairs[block, :] = jnp.concatenate([rh, rl], axis=1)
        s32 = s.astype(F32)
        back = dot(jnp.concatenate([rh, rl, rh], axis=1), b_three, 1, 0)
        dz[block, :] = (back * (1.0 - s32 * s32)).astype(BF)
    save_dz = pltpu.make_async_copy(dz, dz_out, out_sem.at[1])
    save_dz.start()
    both = dot(pairs[...], second[...], 0, 0)
    sums = both[:maps] + both[maps:]
    zero = core == 0
    own, other = jnp.where(zero, sums[:few], sums[few:]), jnp.where(zero, sums[few:], sums[:few])
    for p in range(n_pts):
        cols = slice(2 * p * rows, 2 * (p + 1) * rows)
        s_mine[p] = own[:, cols]
        s_theirs[p] = encode(other[:, cols])
    saves = [save_dz]
    for i in range(4):
        block = slice(i * quarter, (i + 1) * quarter)
        g = dot(first[:, block], dz[...], 0, 0)
        if i < 2:
            near[block, :] = g
            continue
        part = slice((i - 2) * quarter, (i - 1) * quarter)
        far_all[part, :] = encode(g)
        saves.append(
            pltpu.make_async_copy(far_all.at[part, :], far.at[part, :], out_sem.at[i])
        )
        saves[-1].start()
    for save in saves:
        save.wait()


def send_kernel(near, got, low):
    quarter = low.shape[0]
    low[...] = encode(near[quarter:] + decode(got[quarter:]))


def keep_kernel(near, got, after, own):
    quarter = own.shape[0]
    own[...] = near[:quarter] + decode(got[:quarter])


def pack_sums_kernel(mine, got, after, out):
    out[...] = encode(mine[...] + decode(got[...]))


def sums_kernel(scale_b, got, w_both, after, total_out, part):
    total = decode(got[0])
    for p in range(1, got.shape[0]):
        total += decode(got[p])
    total_out[...] = total
    high, low = split(total)
    w = w_both[...]
    part[...] = (dot(high, w, 1, 0) + dot(low, w, 1, 0)) * scale_b


def grad_out_kernel(scale_b, core_ref, mine, theirs, own, other, after, grad_out):
    zero = core_ref[0] == 0
    rows = grad_out.shape[0]
    both = lambda a, b: jnp.concatenate(
        [jnp.where(zero, a[...], b[...]), jnp.where(zero, b[...], a[...])], axis=0
    )
    sums = both(mine, theirs)
    high, low = split(jnp.where(zero, sums[:, :rows], sums[:, rows:]))
    branch = both(own, other)
    grad_out[...] = (dot(high, branch, 0, 0) + dot(low, branch, 0, 0)) * scale_b


def input_kernel(
    place_ref, features_in, near_a, near_b, far_a, far_b, dz_in, after, mine, theirs, done,
    features, grads, w_in, w_mid, dz, sem,
):
    points, hidden = grads.shape
    width, enc = dz.shape[1], features.shape[1]
    quarter, half, step = hidden // 4, hidden // 2, points // 4
    block = lambda i: slice(i * step, (i + 1) * step)
    load_features = pltpu.make_async_copy(features_in, features, sem.at[12])
    load_features.start()
    parts = (near_a, near_b, far_a, far_b)
    to = lambda j: pl.ds(j * quarter, quarter)
    small = [
        pltpu.make_async_copy(part.at[:, pl.ds(width, enc)], w_in.at[to(j), :], sem.at[4 + j])
        for j, part in enumerate(parts)
    ]
    large = [
        pltpu.make_async_copy(part.at[:, pl.ds(0, width)], w_mid.at[to(j), :], sem.at[j])
        for j, part in enumerate(parts)
    ]
    values = [
        pltpu.make_async_copy(dz_in.at[block(i), :], dz.at[block(i), :], sem.at[8 + i])
        for i in range(4)
    ]
    for load in (*small, values[0], *large, *values[1:]):
        load.start()
    load_features.wait()
    for load in small:
        load.wait()
    for i in range(4):
        f = jnp.tanh(dot(features[block(i), :], w_in[...], 1, 1)).astype(BF).astype(F32)
        slope = 1.0 - f * f
        values[i].wait()
        d = dz[block(i), :]
        for j in range(4):
            if i == 0:
                large[j].wait()
            cols = slice(j * quarter, (j + 1) * quarter)
            back = dot(d, w_mid[cols, :], 1, 1)
            grads[block(i), cols] = (back * slope[:, cols]).astype(BF)
    g = dot(features[...], grads[...], 0, 0).T
    done[...] = g[: done.shape[0]]
    n_pts, rows, _ = mine.shape
    for j in range(n_pts):
        p = place_ref[j]
        mine[p] = g[j * rows : (j + 1) * rows]
        theirs[p] = encode(g[half + j * rows : half + (j + 1) * rows])


def pack_last_kernel(part, mine, got, after, out):
    enc = mine.shape[2]
    for p in range(out.shape[0]):
        block = part[p] if part.shape == mine.shape else part[:, p * enc : (p + 1) * enc]
        out[p, :, :enc] = encode(block)
    out[:, :, enc:] = encode(mine[...] + decode(got[...]))


def fold_kernel(own, got, keep, *codes):
    rows = keep.shape[0]
    keep[...] = own[:rows] + decode(got[:rows])
    for k, code in enumerate(codes):
        block = slice((k + 1) * rows, (k + 2) * rows)
        code[...] = encode(own[block] + decode(got[block]))


def hold_kernel(value, after, out):
    out[...] = value[...]


def last_kernel(keep, *refs):
    *codes, grad_mid = refs
    total = keep[...]
    for code in codes:
        total += decode(code[...])
    grad_mid[...] = total


def last_small_kernel(got, grad_branch, grad_in):
    total = decode(got[0])
    for p in range(1, got.shape[0]):
        total += decode(got[p])
    enc = grad_in.shape[1]
    grad_branch[...] = total[:, :enc]
    grad_in[...] = total[:, enc:]


def cost(flops, moved):
    return pl.CostEstimate(flops=int(flops), bytes_accessed=int(moved), transcendentals=0)


def call(kernel, outs, scratch, estimate, spaces, *args, mib=KERNEL_MIB):
    kinds = {"s": pltpu.SMEM, "v": pltpu.VMEM, "h": pltpu.HBM, "a": pl.ANY}
    specs = [pl.BlockSpec(memory_space=kinds[c]) for c in spaces]
    return pl.pallas_call(
        kernel,
        in_specs=specs[: len(args)],
        out_specs=specs[len(args) :],
        out_shape=[jax.ShapeDtypeStruct(shape, dtype) for shape, dtype in outs],
        scratch_shapes=scratch,
        compiler_params=pltpu.CompilerParams(vmem_limit_bytes=mib * MIB),
        cost_estimate=estimate,
    )(*args)


def per_device(features, target, branch, w_in, w_mid, w_out):
    n_pts = lax.axis_size("pts")
    core = lax.axis_index("maps")
    point = lax.axis_index("pts")
    rows, width = w_mid.shape
    hidden = rows * n_pts * 2
    quarter, half = hidden // 4, hidden // 2
    n_hi = n_pts // 2
    maps = 2 * branch.shape[0]
    points, enc = features.shape
    scale_b = 1.0 / math.sqrt(width)
    scale_p = 1.0 / math.sqrt(target.shape[1] * n_pts)
    swap_core = lambda v: lax.ppermute(v, "maps", [(0, 1), (1, 0)])
    move = lambda v, mask: lax.ppermute(v, "pts", [(i, i ^ mask) for i in range(n_pts)])
    exchange = lambda v: lax.all_to_all(v, "pts", 0, 0, tiled=True)
    pick = lambda flag, a, b: jnp.where(flag, a, b)
    first_core = core == 0
    core_ref = core.reshape(1)
    masks = [2 * k + y for y in range(2) for k in range(n_hi)]
    place = point ^ jnp.array(masks, jnp.int32)

    branch_own = branch.reshape(rows, enc)
    (pair,) = call(
        pair_kernel, [((2 * rows, enc), BF)], [], cost(1, 1), "vv" + "v",
        branch_own, move(branch_own, 1),
    )

    (own,) = call(
        beside_kernel, [((rows, width + enc), BF)], [], cost(1, 1), "vv" + "v", w_mid, w_in,
        mib=58,
    )
    (line,) = call(
        stack_kernel, [((quarter, width + enc), BF)], [], cost(1, 1e6), "v" * n_hi + "v",
        own, *[move(own, 2 * k) for k in range(1, n_hi)],
    )
    other = move(line, 1)
    mid = (line, other, swap_core(line), swap_core(other))

    square = width // n_pts == enc
    pairs = [pair] + [move(pair, 2 * k) for k in range(1, n_hi)]
    if not square:
        unmask = point ^ jnp.arange(n_pts, dtype=jnp.int32)
        small = jnp.stack(pairs).reshape(n_pts, *branch.shape)[unmask]
        pairs = [small.transpose(1, 0, 2).reshape(maps // 2, width)]
    (w_both,) = call(
        both_kernel, [((2 * rows, width), BF)], [], cost(5e10, 1), "svva" + "v",
        core_ref, w_out, swap_core(w_out), own,
    )
    folded, wide_own = call(
        functools.partial(fold_branch_kernel, scale_b),
        [((n_pts, maps // 2, 2 * rows), BF), ((maps // 2, width), BF)], [],
        cost(1, 1), "sv" + "v" * len(pairs) + "vv", place, w_both, *pairs,
    )
    b_own = exchange(folded)
    b_other = swap_core(b_own)
    wide_other = swap_core(wide_own)

    t_own = lax.dynamic_slice_in_dim(target, core * points, points, 1)
    t_other = swap_core(lax.dynamic_slice_in_dim(target, (1 - core) * points, points, 1))
    t_full = jnp.concatenate(
        [pick(first_core, t_own, t_other), pick(first_core, t_other, t_own)], axis=0
    ).T

    dma = pltpu.SemaphoreType.DMA
    sums_block = (n_pts, maps // 2, 2 * rows)
    far, near, s_mine, s_theirs, dz = call(
        functools.partial(main_kernel, scale_p),
        [((half, width), BF), ((half, width), F32), (sums_block, F32), (sums_block, BF)]
        + [((points, width), BF)],
        [
            pltpu.VMEM((points, hidden), BF), pltpu.VMEM((points, width), BF),
            pltpu.VMEM((points, width), BF), pltpu.VMEM((hidden, enc), BF),
            pltpu.VMEM((hidden, width), BF), pltpu.VMEM((points, 2 * maps), BF),
            pltpu.VMEM((maps, width), F32),
            pltpu.VMEM((half, width), BF), dma((8,)), dma((4,)),
        ],
        cost(5e10, 8e6), "svhhhhvvv" + "hvvvh",
        core_ref, features, *mid, b_own, b_other, t_full,
        mib=47,
    )

    far_got = swap_core(far)
    (low,) = call(
        send_kernel, [((quarter, width), BF)], [], cost(1, 1), "vv" + "v", near, far_got
    )
    (own,) = call(
        keep_kernel, [((quarter, width), F32)], [], cost(5e10, 1e6), "vva" + "v", near, far_got, low
    )

    (s_code,) = call(
        pack_sums_kernel, [(sums_block, BF)], [], cost(1, 1), "vva" + "v",
        s_mine, swap_core(s_theirs), own,
    )
    in_mine, in_theirs, in_done = call(
        input_kernel, [((n_pts, rows, enc), F32), ((n_pts, rows, enc), BF), ((8, enc), F32)],
        [
            pltpu.VMEM((points, enc), BF), pltpu.VMEM((points, hidden), BF),
            pltpu.VMEM((hidden, enc), BF), pltpu.VMEM((hidden, width), BF),
            pltpu.VMEM((points, width), BF), dma((13,)),
        ],
        cost(5e10, 8e6), "shhhhhha" + "vvv", place, features, *mid, dz, own,
        mib=58,
    )
    total, part = call(
        functools.partial(sums_kernel, scale_b),
        [((maps // 2, 2 * rows), F32), ((maps // 2, width), F32)],
        [], cost(1, 1), "vva" + "vv", exchange(s_code), w_both, in_done,
    )
    if not square:
        part = part.reshape(maps // 2, n_pts, width // n_pts).transpose(1, 0, 2)
        part = part.reshape(n_pts, rows, enc)

    wide_row = (rows, width)
    keep, *codes = call(
        fold_kernel, [(wide_row, F32)] + [(wide_row, BF)] * (n_hi - 1), [], cost(1, 1),
        "vv" + "v" * n_hi, own, move(low, 1),
    )
    (keep,) = call(hold_kernel, [(wide_row, F32)], [], cost(5e10, 1), "va" + "v", keep, codes[0])
    (last,) = call(
        pack_last_kernel, [((n_pts, rows, 2 * enc), BF)], [], cost(1, 1), "vvva" + "v",
        part, in_mine, swap_core(in_theirs), keep,
    )
    (keep,) = call(hold_kernel, [(wide_row, F32)], [], cost(5e10, 1), "va" + "v", keep, last)
    (grad_out,) = call(
        functools.partial(grad_out_kernel, scale_b), [((rows, width), F32)], [], cost(1, 1),
        "svvvva" + "v", core_ref, total, swap_core(total), wide_own, wide_other, keep,
    )
    codes = [move(codes[k], 2 * (k + 1)) for k in reversed(range(len(codes)))]
    (grad_mid,) = call(
        last_kernel, [(wide_row, F32)], [], cost(1, 1), "v" * n_hi + "v", keep, *codes
    )
    grad_branch, grad_in = call(
        last_small_kernel, [((rows, enc), F32), ((rows, enc), F32)],
        [], cost(1, 1), "v" + "vv", exchange(last),
    )
    grad_branch = grad_branch.reshape(maps // 2, width // n_pts).T
    return (grad_branch, grad_in, grad_mid, grad_out)


def solution(mesh):
    in_specs = (
        P(("grp", "pts", "maps"), None),
        P("maps", ("grp", "pts")),
        P(("grp", "maps"), "pts"),
        P(("pts", "maps"), None),
        P(("pts", "maps"), None),
        P(("pts", "maps"), None),
    )
    out_specs = (
        P("pts", ("grp", "maps")),
        P(("grp", "pts", "maps"), None),
        P(("grp", "pts", "maps"), None),
        P(("grp", "pts", "maps"), None),
    )
    return jax.shard_map(
        per_device, mesh=mesh, in_specs=in_specs, out_specs=out_specs, check_vma=False
    )
```
